32 devices in a mesh: blk: 4 (over y, x), rep: 8 (over z, core).
Axes of the slice: x: 2, y: 2, z: 4, core: 2. Of those that a mesh axis runs over, the one named last changes fastest.
Arguments:
- node_feats: bfloat16 [12288, 128], P(('blk', 'rep')), may hold values from -6 to 6
- block_vals: bfloat16 [4, 8, 4, 40, 128, 128], P('blk', 'rep'), may hold values from 0.00049972534 to 0.049804688
- block_rows: int32 [4, 8, 4, 40], P('blk', 'rep'), may hold values from 0 to 23
- block_cols: int32 [4, 8, 4, 40], P('blk', 'rep'), may hold values from 0 to 2
- block_count: int32 [4, 8, 4], P('blk', 'rep'), may hold values from 1 to 40, as said below
- weight: bfloat16 [128, 256], replicated, may hold values from -0.5 to 0.5
Outputs:
- layer_out: bfloat16 [12288, 256], P(('blk', 'rep'))
The draws below stay inside these ranges and needn't reach their ends.
Inputs may be any that keep to these rules, and one draw needn't show every extreme that they name: Only the first block_count[b, r, j] slots of list (b, r, j) are live; the values, rows and columns of later slots are ignored. The largest count 40 is reached in every draw.
All inputs are finite; a program needn't handle non-finite values.
Results may differ from the reference program's by a relative error of at most 0.0011.
Values may be sent and summed in bfloat16 or wider, within the bound.
A program may use at most 128 MiB of HBM per device.

```python
import math
import jax
import jax.numpy as jnp
import numpy as np
from jax import lax

F = 128
H = 256
BS = 128
SLOTS = 40
PIECE_BLK = 3
PANEL_BLK = 24
NODES = 12288
N_BLK = 4
N_REP = 8


def draw_block_count(key, part):
    dims_all = (N_BLK, N_REP, N_BLK)
    total = N_BLK * N_REP * N_BLK
    key_light, key_hubs, key_heavy, key_spot = jax.random.split(key, 4)
    light_load = jax.random.randint(key_light, dims_all, max(1, SLOTS // 8), SLOTS // 3 + 1)
    hub_lists = jax.random.randint(key_hubs, dims_all, 0, 8) == 0
    heavy_load = SLOTS - jax.random.randint(key_heavy, dims_all, 0, max(1, SLOTS // 8))
    counts = jnp.where(hub_lists, heavy_load, light_load)
    hotspot = jax.random.randint(key_spot, (), 0, total)
    flattened = jnp.where(jnp.arange(total) == hotspot, SLOTS, counts.reshape(-1))
    return flattened.reshape(dims_all).astype(jnp.int32)


def with_ends(entries, own_key, smallest, largest):
    shape = entries.shape
    index_at = [jax.random.randint(jax.random.fold_in(own_key, axis), (), 0, shape[axis]) for axis in range(len(shape))]
    entries = entries.at[tuple(index_at)].set(smallest)
    longest = shape.index(max(shape))
    index_at[longest] = (index_at[longest] + 1) % shape[longest]
    return entries.at[tuple(index_at)].set(largest)


def levels(stream_key, dims, shards, low, high):
    gain = 1.0
    for dim, blocks in shards:
        heights = jax.random.uniform(jax.random.fold_in(jax.random.fold_in(stream_key, 6), dim), (blocks,), jnp.float32, low / len(shards), high / len(shards))
        gain = gain * jnp.repeat(jnp.exp(heights), dims[dim] // blocks).reshape((-1,) + (1,) * (len(dims) - 1 - dim))
    return gain


def rank_bounds(amount, skew):
    portions = [(1 << 20) // math.isqrt(rank ** skew) + 1 for rank in range(1, amount + 1)]
    deviation = 1 + sum(portions) // (1 << 30)
    return np.cumsum(np.array([max(1, weight // deviation) for weight in portions]))


def ranked_ids(key, dims, count, slope):
    table = rank_bounds(count, slope)
    lot = jax.random.randint(jax.random.fold_in(key, 1), dims, 0, int(table[count - 1]))
    grade = jnp.searchsorted(jnp.asarray(table, jnp.int32), lot, side="right")
    return jax.random.permutation(jax.random.fold_in(key, 2), count)[grade].astype(jnp.int32)


def noise(stream_key, extent, width, reach, shards=(), kind=jnp.bfloat16):
    drawn = width * jax.random.normal(stream_key, extent, jnp.float32)
    if shards:
        drawn = drawn * levels(stream_key, extent, shards, -0.22, 0.18)
    return jnp.clip(drawn, -reach, reach).astype(kind)


def setup_inputs(seed: int = 0) -> dict:
    arg_keys = jax.random.split(jax.random.key(seed), 7)
    return {
        "node_feats": noise(arg_keys[0], (NODES, F), 1.0, 6.0, ((0, 32),)),
        "block_vals": jnp.clip(jnp.exp(math.log(0.049804688) - 4.6018058 * jax.random.uniform(arg_keys[1], (N_BLK, N_REP, N_BLK, SLOTS, BS, BS), jnp.float32) ** levels(arg_keys[1], (N_BLK, N_REP, N_BLK, SLOTS, BS, BS), ((0, 4), (1, 8)), -0.2, 0.2)), 0.00049972534, 0.049804688).astype(jnp.bfloat16),
        "block_rows": with_ends(ranked_ids(arg_keys[2], (N_BLK, N_REP, N_BLK, SLOTS), PANEL_BLK, 2), jax.random.fold_in(arg_keys[2], 3), 0, PANEL_BLK - 1).astype(jnp.int32),
        "block_cols": with_ends(jax.random.randint(arg_keys[3], (N_BLK, N_REP, N_BLK, SLOTS), 0, PIECE_BLK), jax.random.fold_in(arg_keys[3], 1), 0, PIECE_BLK - 1).astype(jnp.int32),
        "block_count": draw_block_count(jax.random.fold_in(arg_keys[6], 71), 0),
        "weight": noise(arg_keys[5], (F, H), F ** -0.5, 0.5),
    }


def reference(node_feats, block_vals, block_rows, block_cols, block_count, weight):
    pieces = node_feats.reshape(N_BLK, N_REP, PIECE_BLK, BS, F).astype(jnp.float32)
    source = jnp.arange(N_BLK, dtype=jnp.int32)[None, :, None]
    replica = jnp.arange(N_REP, dtype=jnp.int32)[:, None, None]
    slot_ids = jnp.arange(SLOTS, dtype=jnp.int32)

    def one_panel(inputs):
        vals_panel, rows_panel, cols_panel, count_panel = inputs
        gathered = pieces[source, replica, cols_panel]
        products = jnp.einsum("rjsab,rjsbf->rjsaf", vals_panel.astype(jnp.float32), gathered)
        in_use = slot_ids[None, None, :] < count_panel[:, :, None]
        products = jnp.where(in_use[:, :, :, None, None], products, jnp.float32(0.0))
        panel_sum = jnp.zeros((PANEL_BLK, BS, F), jnp.float32)
        panel_sum = panel_sum.at[rows_panel.reshape(-1)].add(products.reshape(-1, BS, F))
        return panel_sum

    panels = lax.map(one_panel, (block_vals, block_rows, block_cols, block_count))
    agg = panels.reshape(NODES, F)
    result = jnp.dot(agg, weight.astype(jnp.float32), precision=lax.Precision.HIGHEST)
    return jnp.maximum(result, 0.0).astype(jnp.bfloat16)
```

```python
import functools

import jax
import jax.numpy as jnp
from jax import lax
from jax.experimental import pallas as pl
from jax.experimental.pallas import tpu as pltpu
from jax.sharding import PartitionSpec as P

BS = 128
LEVELS = 32000.0
STEPS = 256.0
TINY = 1e-36
PAD = 16
MESH = pl.DeviceIdType.MESH


def flip(index, mask, size):
    if size & (size - 1):
        return (index + mask) % size
    out = index
    bit = 1
    while bit < size:
        if mask & bit:
            out = out + bit * (1 - 2 * ((index // bit) % 2))
        bit *= 2
    return out


def back(mask, size):
    return (size - mask) % size if size & (size - 1) else mask


def pack(total, box):
    rows = total.shape[0]
    top = jnp.max(jnp.abs(total), axis=0, keepdims=True)
    code = jnp.ceil(jnp.log2(jnp.maximum(top, TINY)) * STEPS)
    inverse = 1.0 / jnp.exp2(code * (1.0 / STEPS))
    scaled = jnp.round(total * inverse * LEVELS)
    box[pl.ds(0, rows)] = scaled.astype(jnp.int32).astype(jnp.int16)
    box[pl.ds(rows, PAD)] = (
        jnp.broadcast_to(code, (PAD, code.shape[1])).astype(jnp.int32).astype(jnp.int16)
    )


def unpack(box):
    rows = box.shape[0] - PAD
    code = box[pl.ds(rows, PAD)].astype(jnp.int32).astype(jnp.float32)[0:1]
    scale = jnp.exp2(code * (1.0 / STEPS))
    return box[pl.ds(0, rows)].astype(jnp.int32).astype(jnp.float32) * (1.0 / LEVELS) * scale


def kernel(
    n_blk, line, group,
    x_ref, vals_hbm, cols, table, w_ref, out_ref,
    vals, chain, own, sib_send, sib_recv, box_send, up_recv, down_recv,
    vals_sem, x_send_sem, x_recv_sem, sib_send_sem, sib_recv_sem,
    box_send_sem, up_sem, down_sem, *pieces,
):
    slots = vals.shape[1]
    width = x_ref.shape[2]
    blk = lax.axis_index("blk")
    rep = lax.axis_index("rep")
    place = rep // 2
    core = rep % 2
    sibling = {"rep": place * 2 + 1 - core}
    above = {"rep": rep + 2}
    below = {"rep": rep - 2}

    for turn in range(n_blk):
        j = flip(blk, back(turn, n_blk), n_blk)
        load = pltpu.make_async_copy(vals_hbm.at[j], vals.at[j], vals_sem.at[turn])
        load.start()

    barrier = pltpu.get_barrier_semaphore()
    for turn in range(1, n_blk):
        pl.semaphore_signal(
            barrier, inc=1, device_id={"blk": flip(blk, turn, n_blk)}, device_id_type=MESH
        )
    pl.semaphore_signal(barrier, inc=1, device_id=sibling, device_id_type=MESH)

    @pl.when(place < line - 1)
    def _():
        pl.semaphore_signal(barrier, inc=1, device_id=above, device_id_type=MESH)

    @pl.when(place > 0)
    def _():
        pl.semaphore_signal(barrier, inc=1, device_id=below, device_id_type=MESH)

    peers = n_blk + jnp.where(place > 0, 1, 0) + jnp.where(place < line - 1, 1, 0)
    pl.semaphore_wait(barrier, peers)

    sends = []
    for turn in range(1, n_blk):
        send = pltpu.make_async_remote_copy(
            src_ref=x_ref,
            dst_ref=pieces[turn - 1],
            send_sem=x_send_sem.at[turn],
            recv_sem=x_recv_sem.at[turn],
            device_id={"blk": flip(blk, turn, n_blk)},
            device_id_type=MESH,
        )
        send.start()
        sends.append(send)

    chain[n_blk * slots] = jnp.zeros((BS, width), jnp.float32)

    batch = max(u for u in (1, 2, 4, 5, 8) if slots % u == 0)
    for turn in range(n_blk):
        j = flip(blk, back(turn, n_blk), n_blk)
        if turn:
            pltpu.make_async_remote_copy(
                src_ref=x_ref,
                dst_ref=pieces[turn - 1],
                send_sem=x_send_sem.at[turn],
                recv_sem=x_recv_sem.at[turn],
                device_id=sibling,
                device_id_type=MESH,
            ).wait_recv()
        pltpu.make_async_copy(vals_hbm.at[j], vals.at[j], vals_sem.at[turn]).wait()

        piece = pieces[turn - 1] if turn else x_ref

        def some(g, carry, j=j, piece=piece):
            first = g * batch
            products = [
                jnp.dot(
                    vals[j, first + u],
                    piece[cols[j, first + u]],
                    preferred_element_type=jnp.float32,
                )
                for u in range(batch)
            ]
            for u in range(batch):
                chain[j * slots + first + u] = products[u] + chain[table[j, first + u]]
            return carry

        lax.fori_loop(0, slots // batch, some, 0)

    def block_sum(k):
        total = chain[table[0, slots + k]]
        for j in range(1, n_blk):
            total = total + chain[table[j, slots + k]]
        return total

    def sib_copy(d):
        return pltpu.make_async_remote_copy(
            src_ref=sib_send.at[d],
            dst_ref=sib_recv.at[d],
            send_sem=sib_send_sem.at[d],
            recv_sem=sib_recv_sem.at[d],
            device_id=sibling,
            device_id_type=MESH,
        )

    lower = place < line // 2

    def gather(i, carry):
        d = jnp.where(lower, line - 1 - i, i)
        for g in range(group):
            sib_send[d, g * BS:(g + 1) * BS] = block_sum((2 * d + 1 - core) * group + g)
        sib_copy(d).start()
        for g in range(group):
            own[d, g * BS:(g + 1) * BS] = block_sum((2 * d + core) * group + g)
        return carry

    lax.fori_loop(0, line, gather, 0)

    def up_copy(d):
        return pltpu.make_async_remote_copy(
            src_ref=box_send.at[d],
            dst_ref=up_recv.at[d],
            send_sem=box_send_sem.at[d],
            recv_sem=up_sem.at[d],
            device_id=above,
            device_id_type=MESH,
        )

    def down_copy(d):
        return pltpu.make_async_remote_copy(
            src_ref=box_send.at[d],
            dst_ref=down_recv.at[d],
            send_sem=box_send_sem.at[d],
            recv_sem=down_sem.at[d],
            device_id=below,
            device_id_type=MESH,
        )

    def step(s, carry):
        @pl.when(place <= s)
        def _():
            d = line - 1 - s + place
            sib_copy(d).wait_recv()
            own[d] = own[d] + sib_recv[d]

            @pl.when(place > 0)
            def _():
                up_copy(d).wait_recv()
                own[d] = own[d] + unpack(up_recv.at[d])

            pack(own[d], box_send.at[d])
            up_copy(d).start()

        @pl.when(line - 1 - place <= s)
        def _():
            d = s - (line - 1) + place
            sib_copy(d).wait_recv()
            own[d] = own[d] + sib_recv[d]

            @pl.when(place < line - 1)
            def _():
                down_copy(d).wait_recv()
                own[d] = own[d] + unpack(down_recv.at[d])

            pack(own[d], box_send.at[d])
            down_copy(d).start()

        return carry

    lax.fori_loop(0, line - 1, step, 0)

    sib_copy(place).wait_recv()
    own[place] = own[place] + sib_recv[place]

    @pl.when(place > 0)
    def _():
        up_copy(place).wait_recv()
        own[place] = own[place] + unpack(up_recv.at[place])

    @pl.when(place < line - 1)
    def _():
        down_copy(place).wait_recv()
        own[place] = own[place] + unpack(down_recv.at[place])

    total = own[place]
    high = total.astype(jnp.bfloat16)
    low = (total - high.astype(jnp.float32)).astype(jnp.bfloat16)
    w = w_ref[...]
    result = jnp.dot(high, w, preferred_element_type=jnp.float32) + jnp.dot(
        low, w, preferred_element_type=jnp.float32
    )
    out_ref[...] = jnp.maximum(result, 0.0).astype(jnp.bfloat16)

    for send in sends:
        send.wait_send()

    def finish(d, carry):
        sib_copy(d).wait_send()

        @pl.when(d > place)
        def _():
            up_copy(d).wait_send()

        @pl.when(d < place)
        def _():
            down_copy(d).wait_send()

        return carry

    lax.fori_loop(0, line, finish, 0)


def local(node_feats, block_vals, block_rows, block_cols, block_count, weight):
    n_blk = lax.axis_size("blk")
    line = lax.axis_size("rep") // 2
    width = node_feats.shape[1]
    x = node_feats.reshape(-1, BS, width)
    group = x.shape[0]
    vals = block_vals[0, 0]
    rows = block_rows[0, 0]
    cols = block_cols[0, 0]
    count = block_count[0, 0]
    slots = rows.shape[1]
    panel = group * 2 * line

    wanted = jnp.concatenate(
        [rows, jnp.broadcast_to(jnp.arange(panel, dtype=jnp.int32), (n_blk, panel))], axis=1
    )
    spot = jnp.arange(slots, dtype=jnp.int32)
    bound = jnp.minimum(jnp.arange(slots + panel, dtype=jnp.int32), slots)
    hit = (
        (rows[:, None, :] == wanted[:, :, None])
        & (spot[None, None, :] < bound[None, :, None])
        & (spot[None, None, :] < count[:, None, None])
    )
    best = jnp.max(jnp.where(hit, spot[None, None, :], -1), axis=2)
    base = jnp.arange(n_blk, dtype=jnp.int32)[:, None] * slots
    table = jnp.where(best < 0, n_blk * slots, base + best)

    unit = group * BS
    vmem = pl.BlockSpec(memory_space=pltpu.VMEM)
    smem = pl.BlockSpec(memory_space=pltpu.SMEM)
    dma = pltpu.SemaphoreType.DMA
    return pl.pallas_call(
        functools.partial(kernel, n_blk, line, group),
        out_shape=jax.ShapeDtypeStruct((unit, weight.shape[1]), jnp.bfloat16),
        in_specs=[vmem, pl.BlockSpec(memory_space=pl.ANY), smem, smem, vmem],
        out_specs=vmem,
        scratch_shapes=[
            pltpu.VMEM(vals.shape, jnp.bfloat16),
            pltpu.VMEM((n_blk * slots + 1, BS, width), jnp.float32),
            pltpu.VMEM((line, unit, width), jnp.float32),
            pltpu.VMEM((line, unit, width), jnp.float32),
            pltpu.VMEM((line, unit, width), jnp.float32),
            pltpu.VMEM((line, unit + PAD, width), jnp.int16),
            pltpu.VMEM((line, unit + PAD, width), jnp.int16),
            pltpu.VMEM((line, unit + PAD, width), jnp.int16),
            dma((n_blk,)), dma((n_blk,)), dma((n_blk,)),
            dma((line,)), dma((line,)), dma((line,)), dma((line,)), dma((line,)),
        ]
        + [pltpu.VMEM((group, BS, width), jnp.bfloat16)] * (n_blk - 1),
        compiler_params=pltpu.CompilerParams(
            collective_id=0, has_side_effects=True, vmem_limit_bytes=56 * 1024 * 1024
        ),
        cost_estimate=pl.CostEstimate(
            flops=2 * n_blk * slots * BS * BS * width,
            bytes_accessed=2 * n_blk * slots * BS * BS,
            transcendentals=0,
        ),
    )(x, vals, cols, table, weight)


def solution(mesh):
    return jax.shard_map(
        local,
        mesh=mesh,
        in_specs=(
            P(("blk", "rep"), None),
            P("blk", "rep", None, None, None, None),
            P("blk", "rep", None, None),
            P("blk", "rep", None, None),
            P("blk", "rep", None),
            P(),
        ),
        out_specs=P(("blk", "rep"), None),
        check_vma=False,
    )
```

```python
import functools

import jax
import jax.numpy as jnp
from jax import lax
from jax.experimental import pallas as pl
from jax.experimental.pallas import tpu as pltpu
from jax.sharding import PartitionSpec as P

BS = 128
LEVELS = 32000.0
STEPS = 256.0
TINY = 1e-36
PAD = 16
MESH = pl.DeviceIdType.MESH


def flip(index, mask, size):
    if size & (size - 1):
        return (index + mask) % size
    out = index
    bit = 1
    while bit < size:
        if mask & bit:
            out = out + bit * (1 - 2 * ((index // bit) % 2))
        bit *= 2
    return out


def back(mask, size):
    return (size - mask) % size if size & (size - 1) else mask


def pack(total, box):
    rows = total.shape[0]
    top = jnp.max(jnp.abs(total), axis=0, keepdims=True)
    code = jnp.ceil(jnp.log2(jnp.maximum(top, TINY)) * STEPS)
    inverse = 1.0 / jnp.exp2(code * (1.0 / STEPS))
    scaled = jnp.round(total * inverse * LEVELS)
    box[pl.ds(0, rows)] = scaled.astype(jnp.int32).astype(jnp.int16)
    box[pl.ds(rows, PAD)] = (
        jnp.broadcast_to(code, (PAD, code.shape[1])).astype(jnp.int32).astype(jnp.int16)
    )


def unpack(box):
    rows = box.shape[0] - PAD
    code = box[pl.ds(rows, PAD)].astype(jnp.int32).astype(jnp.float32)[0:1]
    scale = jnp.exp2(code * (1.0 / STEPS))
    return box[pl.ds(0, rows)].astype(jnp.int32).astype(jnp.float32) * (1.0 / LEVELS) * scale


def prepare(rows_ref, cols_ref, count, prep, panel):
    lists, slots = rows_ref.shape
    lane = lax.broadcasted_iota(jnp.int32, (slots, slots), 1)
    sub = lax.broadcasted_iota(jnp.int32, (slots, slots), 0)
    place = lax.broadcasted_iota(jnp.int32, (slots, panel), 1)

    def upright(line):
        spread = jnp.broadcast_to(line, (slots, slots))
        return jnp.sum(jnp.where(lane == sub, spread, 0), axis=1, keepdims=True)

    prep[...] = jnp.zeros(prep.shape, jnp.int32)
    for j in range(lists):
        key = jnp.where(lane[0:1] < count[j], rows_ref[j:j + 1, :], panel)
        unique = key * slots + lane[0:1]
        key_up = upright(key)
        col_up = upright(cols_ref[j:j + 1, :])
        unique_up = key_up * slots + sub[:, 0:1]
        rank = jnp.sum(jnp.where(unique < unique_up, 1, 0), axis=1, keepdims=True)
        again = jnp.logical_and(key == key_up, lane < sub)
        keep_up = jnp.max(jnp.where(again, 1, 0), axis=1, keepdims=True)
        here = rank == lane
        for at, entry in enumerate((sub, col_up, keep_up)):
            prep[j, at:at + 1, 0:slots] = jnp.sum(
                jnp.where(here, entry, 0), axis=0, keepdims=True
            )
        upto = jnp.sum(jnp.where(key_up <= place, 1, 0), axis=0, keepdims=True)
        found = jnp.max(jnp.where(key_up == place, 1, 0), axis=0, keepdims=True)
        prep[j, 3:4, 0:panel] = jnp.where(found > 0, upto + (j * slots - 1), lists * slots)


def kernel(
    n_blk, line, group,
    x_ref, vals_hbm, rows_ref, cols_ref, count, w_ref, out_ref,
    prep, table, chain, own, sib_send, sib_recv, box_send, up_recv, down_recv,
    vals_sem, x_send_sem, x_recv_sem, sib_send_sem, sib_recv_sem,
    box_send_sem, up_sem, down_sem, table_sem, *pieces_and_vals,
):
    pieces = (x_ref,) + pieces_and_vals[:n_blk - 1]
    vals = pieces_and_vals[n_blk - 1:]
    slots = vals_hbm.shape[1]
    width = x_ref.shape[2]
    blk = lax.axis_index("blk")
    rep = lax.axis_index("rep")
    place = rep // 2
    core = rep % 2
    sibling = {"rep": place * 2 + 1 - core}
    above = {"rep": rep + 2}
    below = {"rep": rep - 2}

    for turn in range(n_blk):
        j = flip(blk, back(turn, n_blk), n_blk)
        load = pltpu.make_async_copy(vals_hbm.at[j], vals[turn], vals_sem.at[turn])
        load.start()

    barrier = pltpu.get_barrier_semaphore()
    for turn in range(1, n_blk):
        pl.semaphore_signal(
            barrier, inc=1, device_id={"blk": flip(blk, turn, n_blk)}, device_id_type=MESH
        )
    pl.semaphore_signal(barrier, inc=1, device_id=sibling, device_id_type=MESH)

    @pl.when(place < line - 1)
    def _():
        pl.semaphore_signal(barrier, inc=1, device_id=above, device_id_type=MESH)

    @pl.when(place > 0)
    def _():
        pl.semaphore_signal(barrier, inc=1, device_id=below, device_id_type=MESH)

    prepare(rows_ref, cols_ref, count, prep, group * 2 * line)
    fill = pltpu.make_async_copy(prep, table, table_sem)
    fill.start()

    peers = n_blk + jnp.where(place > 0, 1, 0) + jnp.where(place < line - 1, 1, 0)
    pl.semaphore_wait(barrier, peers)

    sends = []
    for turn in range(1, n_blk):
        send = pltpu.make_async_remote_copy(
            src_ref=x_ref,
            dst_ref=pieces[turn],
            send_sem=x_send_sem.at[turn],
            recv_sem=x_recv_sem.at[turn],
            device_id={"blk": flip(blk, turn, n_blk)},
            device_id_type=MESH,
        )
        send.start()
        sends.append(send)

    chain[n_blk * slots] = jnp.zeros((BS, width), jnp.float32)

    fill.wait()
    batch = max(u for u in range(1, 21) if slots % u == 0)
    for turn in range(n_blk):
        j = flip(blk, back(turn, n_blk), n_blk)
        pltpu.make_async_copy(vals_hbm.at[j], vals[turn], vals_sem.at[turn]).wait()
        if turn:
            pltpu.make_async_remote_copy(
                src_ref=x_ref,
                dst_ref=pieces[turn],
                send_sem=x_send_sem.at[turn],
                recv_sem=x_recv_sem.at[turn],
                device_id=sibling,
                device_id_type=MESH,
            ).wait_recv()

        def some(g, total, j=j, piece=pieces[turn], blocks=vals[turn]):
            for u in range(batch):
                t = g * batch + u
                product = jnp.dot(
                    blocks[table[j, 0, t]],
                    piece[table[j, 1, t]],
                    preferred_element_type=jnp.float32,
                )
                total = total * table[j, 2, t].astype(jnp.float32) + product
                chain[j * slots + t] = total
            return total

        lax.fori_loop(0, slots // batch, some, jnp.zeros((BS, width), jnp.float32))

    def block_sum(k):
        total = chain[table[0, 3, k]]
        for j in range(1, n_blk):
            total = total + chain[table[j, 3, k]]
        return total

    def sib_copy(d):
        return pltpu.make_async_remote_copy(
            src_ref=sib_send.at[d],
            dst_ref=sib_recv.at[d],
            send_sem=sib_send_sem.at[d],
            recv_sem=sib_recv_sem.at[d],
            device_id=sibling,
            device_id_type=MESH,
        )

    lower = place < line // 2

    def gather(i, carry):
        d = jnp.where(lower, line - 1 - i, i)
        for g in range(group):
            sib_send[d, g * BS:(g + 1) * BS] = block_sum((2 * d + 1 - core) * group + g)
        sib_copy(d).start()
        for g in range(group):
            own[d, g * BS:(g + 1) * BS] = block_sum((2 * d + core) * group + g)
        return carry

    lax.fori_loop(0, line, gather, 0)

    def up_copy(d):
        return pltpu.make_async_remote_copy(
            src_ref=box_send.at[d],
            dst_ref=up_recv.at[d],
            send_sem=box_send_sem.at[d],
            recv_sem=up_sem.at[d],
            device_id=above,
            device_id_type=MESH,
        )

    def down_copy(d):
        return pltpu.make_async_remote_copy(
            src_ref=box_send.at[d],
            dst_ref=down_recv.at[d],
            send_sem=box_send_sem.at[d],
            recv_sem=down_sem.at[d],
            device_id=below,
            device_id_type=MESH,
        )

    def step(s, carry):
        @pl.when(place <= s)
        def _():
            d = line - 1 - s + place
            sib_copy(d).wait_recv()
            own[d] = own[d] + sib_recv[d]

            @pl.when(place > 0)
            def _():
                up_copy(d).wait_recv()
                own[d] = own[d] + unpack(up_recv.at[d])

            pack(own[d], box_send.at[d])
            up_copy(d).start()

        @pl.when(line - 1 - place <= s)
        def _():
            d = s - (line - 1) + place
            sib_copy(d).wait_recv()
            own[d] = own[d] + sib_recv[d]

            @pl.when(place < line - 1)
            def _():
                down_copy(d).wait_recv()
                own[d] = own[d] + unpack(down_recv.at[d])

            pack(own[d], box_send.at[d])
            down_copy(d).start()

        return carry

    lax.fori_loop(0, line - 1, step, 0)

    sib_copy(place).wait_recv()
    own[place] = own[place] + sib_recv[place]

    @pl.when(place > 0)
    def _():
        up_copy(place).wait_recv()
        own[place] = own[place] + unpack(up_recv.at[place])

    @pl.when(place < line - 1)
    def _():
        down_copy(place).wait_recv()
        own[place] = own[place] + unpack(down_recv.at[place])

    total = own[place]
    high = total.astype(jnp.bfloat16)
    low = (total - high.astype(jnp.float32)).astype(jnp.bfloat16)
    w = w_ref[...]
    result = jnp.dot(high, w, preferred_element_type=jnp.float32) + jnp.dot(
        low, w, preferred_element_type=jnp.float32
    )
    out_ref[...] = jnp.maximum(result, 0.0).astype(jnp.bfloat16)

    for send in sends:
        send.wait_send()

    def finish(d, carry):
        sib_copy(d).wait_send()

        @pl.when(d > place)
        def _():
            up_copy(d).wait_send()

        @pl.when(d < place)
        def _():
            down_copy(d).wait_send()

        return carry

    lax.fori_loop(0, line, finish, 0)


def local(node_feats, block_vals, block_rows, block_cols, block_count, weight):
    n_blk = lax.axis_size("blk")
    line = lax.axis_size("rep") // 2
    width = node_feats.shape[1]
    x = node_feats.reshape(-1, BS, width)
    group = x.shape[0]
    vals = block_vals[0, 0]
    rows = block_rows[0, 0]
    cols = block_cols[0, 0]
    count = block_count[0, 0]
    slots = rows.shape[1]
    unit = group * BS
    vmem = pl.BlockSpec(memory_space=pltpu.VMEM)
    smem = pl.BlockSpec(memory_space=pltpu.SMEM)
    dma = pltpu.SemaphoreType.DMA
    return pl.pallas_call(
        functools.partial(kernel, n_blk, line, group),
        out_shape=jax.ShapeDtypeStruct((unit, weight.shape[1]), jnp.bfloat16),
        in_specs=[vmem, pl.BlockSpec(memory_space=pl.ANY), vmem, vmem, smem, vmem],
        out_specs=vmem,
        scratch_shapes=[
            pltpu.VMEM((n_blk, 8, 128), jnp.int32),
            pltpu.SMEM((n_blk, 8, 128), jnp.int32),
            pltpu.VMEM((n_blk * slots + 1, BS, width), jnp.float32),
            pltpu.VMEM((line, unit, width), jnp.float32),
            pltpu.VMEM((line, unit, width), jnp.float32),
            pltpu.VMEM((line, unit, width), jnp.float32),
            pltpu.VMEM((line, unit + PAD, width), jnp.int16),
            pltpu.VMEM((line, unit + PAD, width), jnp.int16),
            pltpu.VMEM((line, unit + PAD, width), jnp.int16),
            dma((n_blk,)), dma((n_blk,)), dma((n_blk,)),
            dma((line,)), dma((line,)), dma((line,)), dma((line,)), dma((line,)),
            dma,
        ]
        + [pltpu.VMEM((group, BS, width), jnp.bfloat16)] * (n_blk - 1)
        + [pltpu.VMEM(vals.shape[1:], jnp.bfloat16)] * n_blk,
        compiler_params=pltpu.CompilerParams(
            collective_id=0, has_side_effects=True, vmem_limit_bytes=56 * 1024 * 1024
        ),
        cost_estimate=pl.CostEstimate(
            flops=2 * n_blk * slots * BS * BS * width,
            bytes_accessed=2 * n_blk * slots * BS * BS,
            transcendentals=0,
        ),
    )(x, vals, rows, cols, count, weight)


def solution(mesh):
    return jax.shard_map(
        local,
        mesh=mesh,
        in_specs=(
            P(("blk", "rep"), None),
            P("blk", "rep", None, None, None, None),
            P("blk", "rep", None, None),
            P("blk", "rep", None, None),
            P("blk", "rep", None),
            P(),
        ),
        out_specs=P(("blk", "rep"), None),
        check_vma=False,
    )
```

```python
import functools

import jax
import jax.numpy as jnp
from jax import lax
from jax.experimental import pallas as pl
from jax.experimental.pallas import tpu as pltpu
from jax.sharding import PartitionSpec as P

BS = 128
LEVELS = 32000.0
STEPS = 256.0
TINY = 1e-36
PAD = 16
MESH = pl.DeviceIdType.MESH


def flip(index, mask, size):
    if size & (size - 1):
        return (index + mask) % size
    out = index
    bit = 1
    while bit < size:
        if mask & bit:
            out = out + bit * (1 - 2 * ((index // bit) % 2))
        bit *= 2
    return out


def back(mask, size):
    return (size - mask) % size if size & (size - 1) else mask


def scale_of(code):
    return jnp.exp2(code * (1.0 / STEPS))


def read_code(box):
    return box[pl.ds(0, PAD)].astype(jnp.int32).astype(jnp.float32)[0:1]


def decode(box, g, scale):
    part = box[pl.ds(PAD + g * BS, BS)].astype(jnp.int32).astype(jnp.float32)
    return part * (1.0 / LEVELS) * scale


def prepare(rows_ref, cols_ref, count_ref, prep, panel, group):
    lists, slots = rows_ref.shape
    lane = lax.broadcasted_iota(jnp.int32, (slots, slots), 1)
    sub = lax.broadcasted_iota(jnp.int32, (slots, slots), 0)
    place = lax.broadcasted_iota(jnp.int32, (slots, panel), 1)
    col_bits = max(1, (group - 1).bit_length())
    slot_bits = max(1, (slots - 1).bit_length())
    row_bits = col_bits + slot_bits

    for j in range(lists):
        live = lane[0:1] < count_ref[0:1, j:j + 1]
        key = jnp.where(live, rows_ref[j:j + 1, :], panel)
        col = jnp.where(live, cols_ref[j:j + 1, :], 0)
        word = key * (1 << row_bits) + lane[0:1] * (1 << col_bits) + col
        spread = jnp.broadcast_to(word, (slots, slots))
        word_up = jnp.sum(jnp.where(lane == sub, spread, 0), axis=1, keepdims=True)
        rank = jnp.sum(jnp.where(word < word_up, 1, 0), axis=1, keepdims=True)
        key_up = word_up >> row_bits
        before = jnp.max(jnp.where(rank == lane - 1, key_up, -1), axis=0, keepdims=True)
        ordered = jnp.sum(jnp.where(rank == lane, word_up, 0), axis=0, keepdims=True)
        prep[j, 0:1, 0:slots] = (ordered >> col_bits) & ((1 << slot_bits) - 1)
        prep[j, 1:2, 0:slots] = ordered & ((1 << col_bits) - 1)
        prep[j, 2:3, 0:slots] = jnp.where(before == (ordered >> row_bits), 1, 0)
        upto = jnp.sum(jnp.where(key_up <= place, 1, 0), axis=0, keepdims=True)
        found = jnp.max(jnp.where(key_up == place, 1, 0), axis=0, keepdims=True)
        prep[j, 3:4, 0:panel] = jnp.where(found > 0, upto + (j * slots - 1), lists * slots)


def kernel(
    n_blk, line, group,
    x_hbm, vals_hbm, rows_hbm, cols_hbm, count_hbm, w_hbm, out_ref,
    rows_ref, cols_ref, count_ref, w_ref, prep, table, chain, own, sib_send, sib_recv, box_send, up_recv, down_recv,
    vals_sem, x_send_sem, x_recv_sem, sib_send_sem, sib_recv_sem,
    box_send_sem, up_sem, down_sem, table_sem, in_sem, *pieces_and_vals,
):
    pieces = pieces_and_vals[:n_blk]
    vals = pieces_and_vals[n_blk:]
    slots = vals_hbm.shape[1]
    width = x_hbm.shape[2]
    blk = lax.axis_index("blk")
    rep = lax.axis_index("rep")
    place = rep // 2
    core = rep % 2
    sibling = {"rep": place * 2 + 1 - core}
    above = {"rep": rep + 2}
    below = {"rep": rep - 2}

    barrier = pltpu.get_barrier_semaphore()
    for turn in range(1, n_blk):
        pl.semaphore_signal(
            barrier, inc=1, device_id={"blk": flip(blk, turn, n_blk)}, device_id_type=MESH
        )
    pl.semaphore_signal(barrier, inc=1, device_id=sibling, device_id_type=MESH)

    @pl.when(place < line - 1)
    def _():
        pl.semaphore_signal(barrier, inc=1, device_id=above, device_id_type=MESH)

    @pl.when(place > 0)
    def _():
        pl.semaphore_signal(barrier, inc=1, device_id=below, device_id_type=MESH)

    fetches = [
        pltpu.make_async_copy(source, target, in_sem.at[i])
        for i, (source, target) in enumerate((
            (rows_hbm, rows_ref),
            (cols_hbm, cols_ref),
            (count_hbm, count_ref),
            (x_hbm, pieces[0]),
            (w_hbm, w_ref),
        ))
    ]
    for fetch in fetches:
        fetch.start()

    for turn in range(n_blk):
        j = flip(blk, back(turn, n_blk), n_blk)
        load = pltpu.make_async_copy(vals_hbm.at[j], vals[turn], vals_sem.at[turn])
        load.start()

    peers = n_blk + jnp.where(place > 0, 1, 0) + jnp.where(place < line - 1, 1, 0)
    pl.semaphore_wait(barrier, peers)

    sends = []
    for turn in range(1, n_blk):
        send = pltpu.make_async_remote_copy(
            src_ref=x_hbm,
            dst_ref=pieces[turn],
            send_sem=x_send_sem.at[turn],
            recv_sem=x_recv_sem.at[turn],
            device_id={"blk": flip(blk, turn, n_blk)},
            device_id_type=MESH,
        )
        send.start()
        sends.append(send)

    prep[...] = jnp.zeros(prep.shape, jnp.int32)
    for fetch in fetches[:3]:
        fetch.wait()
    prepare(rows_ref, cols_ref, count_ref, prep, group * 2 * line, group)
    fill = pltpu.make_async_copy(prep, table, table_sem)
    fill.start()
    chain[n_blk * slots] = jnp.zeros((BS, width), jnp.float32)

    fill.wait()
    for fetch in fetches[3:]:
        fetch.wait()
    batch = max(u for u in range(1, 21) if slots % u == 0)
    for turn in range(n_blk):
        j = flip(blk, back(turn, n_blk), n_blk)
        pltpu.make_async_copy(vals_hbm.at[j], vals[turn], vals_sem.at[turn]).wait()
        if turn:
            pltpu.make_async_remote_copy(
                src_ref=x_hbm,
                dst_ref=pieces[turn],
                send_sem=x_send_sem.at[turn],
                recv_sem=x_recv_sem.at[turn],
                device_id=sibling,
                device_id_type=MESH,
            ).wait_recv()

        def some(g, total, j=j, piece=pieces[turn], blocks=vals[turn]):
            for u in range(batch):
                t = g * batch + u
                product = jnp.dot(
                    blocks[table[j, 0, t]],
                    piece[table[j, 1, t]],
                    preferred_element_type=jnp.float32,
                )
                total = total * table[j, 2, t].astype(jnp.float32) + product
                chain[j * slots + t] = total
            return total

        lax.fori_loop(0, slots // batch, some, jnp.zeros((BS, width), jnp.float32))

    def block_sum(k):
        total = chain[table[0, 3, k]]
        for j in range(1, n_blk):
            total = total + chain[table[j, 3, k]]
        return total

    def sib_copy(d):
        return pltpu.make_async_remote_copy(
            src_ref=sib_send.at[d],
            dst_ref=sib_recv.at[d],
            send_sem=sib_send_sem.at[d],
            recv_sem=sib_recv_sem.at[d],
            device_id=sibling,
            device_id_type=MESH,
        )

    lower = place < line // 2

    def gather(i, carry):
        d = jnp.where(lower, line - 1 - i, i)
        for g in range(group):
            sib_send[d, g * BS:(g + 1) * BS] = block_sum((2 * d + 1 - core) * group + g)
        sib_copy(d).start()
        for g in range(group):
            own[d, g * BS:(g + 1) * BS] = block_sum((2 * d + core) * group + g)
        return carry

    lax.fori_loop(0, line, gather, 0)

    def rows_of(g):
        return pl.ds(0, PAD + BS) if g == 0 else pl.ds(PAD + g * BS, BS)

    def up_copy(d, g):
        return pltpu.make_async_remote_copy(
            src_ref=box_send.at[d, rows_of(g)],
            dst_ref=up_recv.at[d, rows_of(g)],
            send_sem=box_send_sem.at[d, g],
            recv_sem=up_sem.at[d, g],
            device_id=above,
            device_id_type=MESH,
        )

    def down_copy(d, g):
        return pltpu.make_async_remote_copy(
            src_ref=box_send.at[d, rows_of(g)],
            dst_ref=down_recv.at[d, rows_of(g)],
            send_sem=box_send_sem.at[d, g],
            recv_sem=down_sem.at[d, g],
            device_id=below,
            device_id_type=MESH,
        )

    def hop(d, copy, box, first):
        sib_copy(d).wait_recv()
        both = own[d] + sib_recv[d]
        own[d] = both
        top = jnp.max(jnp.abs(both), axis=0, keepdims=True)
        if not first:
            copy(d, 0).wait_recv()
            scale = scale_of(read_code(box.at[d]))
            top = top + scale
        code = jnp.ceil(jnp.log2(jnp.maximum(top, TINY)) * STEPS)
        inverse = 1.0 / scale_of(code)
        box_send[d, 0:PAD] = (
            jnp.broadcast_to(code, (PAD, width)).astype(jnp.int32).astype(jnp.int16)
        )
        for g in range(group):
            total = own[d, g * BS:(g + 1) * BS]
            if not first:
                if g:
                    copy(d, g).wait_recv()
                total = total + decode(box.at[d], g, scale)
            whole = jnp.round(total * inverse * LEVELS).astype(jnp.int32)
            box_send[d, PAD + g * BS:PAD + (g + 1) * BS] = whole.astype(jnp.int16)
            copy(d, g).start()

    def step(s, carry):
        up_to = line - 1 - s + place
        down_to = s - (line - 1) + place

        @pl.when(jnp.logical_and(place <= s, place == 0))
        def _():
            hop(up_to, up_copy, up_recv, True)

        @pl.when(jnp.logical_and(place <= s, place > 0))
        def _():
            hop(up_to, up_copy, up_recv, False)

        @pl.when(jnp.logical_and(line - 1 - place <= s, place == line - 1))
        def _():
            hop(down_to, down_copy, down_recv, True)

        @pl.when(jnp.logical_and(line - 1 - place <= s, place < line - 1))
        def _():
            hop(down_to, down_copy, down_recv, False)

        return carry

    lax.fori_loop(0, line - 1, step, 0)

    sib_copy(place).wait_recv()
    own[place] = own[place] + sib_recv[place]
    w = w_ref[...]
    for g in range(group):
        block = pl.ds(g * BS, BS)

        @pl.when(place > 0)
        def _():
            up_copy(place, g).wait_recv()
            scale = scale_of(read_code(up_recv.at[place]))
            own[place, block] = own[place, block] + decode(up_recv.at[place], g, scale)

        @pl.when(place < line - 1)
        def _():
            down_copy(place, g).wait_recv()
            scale = scale_of(read_code(down_recv.at[place]))
            own[place, block] = own[place, block] + decode(down_recv.at[place], g, scale)

        total = own[place, block]
        high = total.astype(jnp.bfloat16)
        low = (total - high.astype(jnp.float32)).astype(jnp.bfloat16)
        result = jnp.dot(high, w, preferred_element_type=jnp.float32) + jnp.dot(
            low, w, preferred_element_type=jnp.float32
        )
        out_ref[block] = jnp.maximum(result, 0.0).astype(jnp.bfloat16)

    for send in sends:
        send.wait_send()

    def finish(d, carry):
        sib_copy(d).wait_send()

        @pl.when(d > place)
        def _():
            for g in range(group):
                up_copy(d, g).wait_send()

        @pl.when(d < place)
        def _():
            for g in range(group):
                down_copy(d, g).wait_send()

        return carry

    lax.fori_loop(0, line, finish, 0)


def local(node_feats, block_vals, block_rows, block_cols, block_count, weight):
    n_blk = lax.axis_size("blk")
    line = lax.axis_size("rep") // 2
    width = node_feats.shape[1]
    x = node_feats.reshape(-1, BS, width)
    group = x.shape[0]
    vals = block_vals[0, 0]
    rows = block_rows[0, 0]
    cols = block_cols[0, 0]
    count = block_count[0]
    slots = rows.shape[1]
    unit = group * BS
    vmem = pl.BlockSpec(memory_space=pltpu.VMEM)
    anywhere = pl.BlockSpec(memory_space=pl.ANY)
    dma = pltpu.SemaphoreType.DMA
    return pl.pallas_call(
        functools.partial(kernel, n_blk, line, group),
        out_shape=jax.ShapeDtypeStruct((unit, weight.shape[1]), jnp.bfloat16),
        in_specs=[anywhere] * 6,
        out_specs=vmem,
        scratch_shapes=[
            pltpu.VMEM(rows.shape, jnp.int32),
            pltpu.VMEM(cols.shape, jnp.int32),
            pltpu.VMEM(count.shape, jnp.int32),
            pltpu.VMEM(weight.shape, jnp.bfloat16),
            pltpu.VMEM((n_blk, 8, 128), jnp.int32),
            pltpu.SMEM((n_blk, 8, 128), jnp.int32),
            pltpu.VMEM((n_blk * slots + 1, BS, width), jnp.float32),
            pltpu.VMEM((line, unit, width), jnp.float32),
            pltpu.VMEM((line, unit, width), jnp.float32),
            pltpu.VMEM((line, unit, width), jnp.float32),
            pltpu.VMEM((line, unit + PAD, width), jnp.int16),
            pltpu.VMEM((line, unit + PAD, width), jnp.int16),
            pltpu.VMEM((line, unit + PAD, width), jnp.int16),
            dma((n_blk,)), dma((n_blk,)), dma((n_blk,)),
            dma((line,)), dma((line,)),
            dma((line, group)), dma((line, group)), dma((line, group)),
            dma, dma((5,)),
        ]
        + [pltpu.VMEM((group, BS, width), jnp.bfloat16)] * n_blk
        + [pltpu.VMEM(vals.shape[1:], jnp.bfloat16)] * n_blk,
        compiler_params=pltpu.CompilerParams(
            collective_id=0, has_side_effects=True, vmem_limit_bytes=56 * 1024 * 1024
        ),
        cost_estimate=pl.CostEstimate(
            flops=2 * n_blk * slots * BS * BS * width,
            bytes_accessed=2 * n_blk * slots * BS * BS,
            transcendentals=0,
        ),
    )(x, vals, rows, cols, count, weight)


def solution(mesh):
    return jax.shard_map(
        local,
        mesh=mesh,
        in_specs=(
            P(("blk", "rep"), None),
            P("blk", "rep", None, None, None, None),
            P("blk", "rep", None, None),
            P("blk", "rep", None, None),
            P("blk", "rep", None),
            P(),
        ),
        out_specs=P(("blk", "rep"), None),
        check_vma=False,
    )
```

```python
import functools

import jax
import jax.numpy as jnp
from jax import lax
from jax.experimental import pallas as pl
from jax.experimental.pallas import tpu as pltpu
from jax.sharding import PartitionSpec as P

BS = 128
LEVELS = 32000.0
STEPS = 256.0
TINY = 1e-36
PAD = 16
MESH = pl.DeviceIdType.MESH


def flip(index, mask, size):
    if size & (size - 1):
        return (index + mask) % size
    out = index
    bit = 1
    while bit < size:
        if mask & bit:
            out = out + bit * (1 - 2 * ((index // bit) % 2))
        bit *= 2
    return out


def back(mask, size):
    return (size - mask) % size if size & (size - 1) else mask


def scale_of(code):
    return jnp.exp2(code * (1.0 / STEPS))


def read_code(box):
    return box[pl.ds(0, PAD)].astype(jnp.int32).astype(jnp.float32)[0:1]


def decode(box, g, scale):
    part = box[pl.ds(PAD + g * BS, BS)].astype(jnp.int32).astype(jnp.float32)
    return part * (1.0 / LEVELS) * scale


def prepare(rows_ref, cols_ref, count_ref, prep, panel, group):
    lists, slots = rows_ref.shape
    lane = lax.broadcasted_iota(jnp.int32, (slots, slots), 1)
    sub = lax.broadcasted_iota(jnp.int32, (slots, slots), 0)
    place = lax.broadcasted_iota(jnp.int32, (slots, panel), 1)
    col_bits = max(1, (group - 1).bit_length())
    slot_bits = max(1, (slots - 1).bit_length())
    row_bits = col_bits + slot_bits

    for j in range(lists):
        live = lane[0:1] < count_ref[0:1, j:j + 1]
        key = jnp.where(live, rows_ref[j:j + 1, :], panel)
        col = jnp.where(live, cols_ref[j:j + 1, :], 0)
        word = key * (1 << row_bits) + lane[0:1] * (1 << col_bits) + col
        spread = jnp.broadcast_to(word, (slots, slots))
        word_up = jnp.sum(jnp.where(lane == sub, spread, 0), axis=1, keepdims=True)
        rank = jnp.sum(jnp.where(word < word_up, 1, 0), axis=1, keepdims=True)
        key_up = word_up >> row_bits
        before = jnp.max(jnp.where(rank == lane - 1, key_up, -1), axis=0, keepdims=True)
        ordered = jnp.sum(jnp.where(rank == lane, word_up, 0), axis=0, keepdims=True)
        prep[j, 0:1, 0:slots] = (ordered >> col_bits) & ((1 << slot_bits) - 1)
        prep[j, 1:2, 0:slots] = ordered & ((1 << col_bits) - 1)
        prep[j, 2:3, 0:slots] = jnp.where(before == (ordered >> row_bits), 1, 0)
        upto = jnp.sum(jnp.where(key_up <= place, 1, 0), axis=0, keepdims=True)
        found = jnp.max(jnp.where(key_up == place, 1, 0), axis=0, keepdims=True)
        prep[j, 3:4, 0:panel] = jnp.where(found > 0, upto + (j * slots - 1), lists * slots)


def kernel(
    n_blk, line, group,
    x_hbm, vals_hbm, rows_hbm, cols_hbm, count_hbm, w_hbm, out_ref,
    rows_ref, cols_ref, count_ref, w_ref, prep, table, chain, own, sib_send, sib_recv, box_send, up_recv, down_recv,
    vals_sem, x_send_sem, x_recv_sem, sib_send_sem, sib_recv_sem,
    box_send_sem, up_sem, down_sem, table_sem, in_sem, *pieces_and_vals,
):
    pieces = pieces_and_vals[:n_blk]
    vals = pieces_and_vals[n_blk:]
    slots = vals_hbm.shape[1]
    width = x_hbm.shape[2]
    blk = lax.axis_index("blk")
    rep = lax.axis_index("rep")
    place = rep // 2
    core = rep % 2
    sibling = {"rep": place * 2 + 1 - core}
    above = {"rep": rep + 2}
    below = {"rep": rep - 2}

    square = n_blk == 4
    direct = (1, 2) if square else tuple(range(1, n_blk))

    barrier = pltpu.get_barrier_semaphore()
    for turn in direct:
        pl.semaphore_signal(
            barrier, inc=1, device_id={"blk": flip(blk, turn, n_blk)}, device_id_type=MESH
        )
    pl.semaphore_signal(barrier, inc=1, device_id=sibling, device_id_type=MESH)

    @pl.when(place < line - 1)
    def _():
        pl.semaphore_signal(barrier, inc=1, device_id=above, device_id_type=MESH)

    @pl.when(place > 0)
    def _():
        pl.semaphore_signal(barrier, inc=1, device_id=below, device_id_type=MESH)

    fetches = [
        pltpu.make_async_copy(source, target, in_sem.at[i])
        for i, (source, target) in enumerate((
            (rows_hbm, rows_ref),
            (cols_hbm, cols_ref),
            (count_hbm, count_ref),
            (x_hbm, pieces[0]),
            (w_hbm, w_ref),
        ))
    ]
    for fetch in fetches:
        fetch.start()

    def load(turn):
        j = flip(blk, back(turn, n_blk), n_blk)
        return pltpu.make_async_copy(vals_hbm.at[j], vals[turn], vals_sem.at[turn])

    load(0).start()

    peers = len(direct) + 1 + jnp.where(place > 0, 1, 0) + jnp.where(place < line - 1, 1, 0)
    pl.semaphore_wait(barrier, peers)

    def half(ref, h):
        return ref.at[:, pl.ds(h * (BS // 2), BS // 2)]

    def pass_on(source, turn, h, to):
        return pltpu.make_async_remote_copy(
            src_ref=half(source, h),
            dst_ref=half(pieces[turn], h),
            send_sem=x_send_sem.at[turn, h],
            recv_sem=x_recv_sem.at[turn, h],
            device_id={"blk": flip(blk, to, n_blk)},
            device_id_type=MESH,
        )

    sends = [
        pass_on(x_hbm, turn, (first + turn + 1) % 2, turn) for first in (0, 1) for turn in direct
    ]
    for send in sends:
        send.start()
    for turn in range(1, n_blk):
        load(turn).start()

    prep[...] = jnp.zeros(prep.shape, jnp.int32)
    for fetch in fetches[:3]:
        fetch.wait()
    prepare(rows_ref, cols_ref, count_ref, prep, group * 2 * line, group)
    fill = pltpu.make_async_copy(prep, table, table_sem)
    fill.start()
    chain[n_blk * slots] = jnp.zeros((BS, width), jnp.float32)

    fill.wait()
    for fetch in fetches[3:]:
        fetch.wait()
    batch = max(u for u in range(1, 21) if slots % u == 0)
    for turn in range(n_blk):
        j = flip(blk, back(turn, n_blk), n_blk)
        if square and turn == 1:
            for near, h in ((1, 0), (2, 1)):
                pass_on(x_hbm, near, h, near).wait_recv()
                onward = pass_on(pieces[near], 3, h, 3 - near)
                onward.start()
                sends.append(onward)
        load(turn).wait()
        for h in (0, 1) if turn else ():
            if not (square and h == turn - 1):
                pass_on(x_hbm, turn, h, direct[0]).wait_recv()

        def some(g, total, j=j, piece=pieces[turn], blocks=vals[turn]):
            for u in range(batch):
                t = g * batch + u
                product = jnp.dot(
                    blocks[table[j, 0, t]],
                    piece[table[j, 1, t]],
                    preferred_element_type=jnp.float32,
                )
                total = total * table[j, 2, t].astype(jnp.float32) + product
                chain[j * slots + t] = total
            return total

        lax.fori_loop(0, slots // batch, some, jnp.zeros((BS, width), jnp.float32))

    def block_sum(k):
        total = chain[table[0, 3, k]]
        for j in range(1, n_blk):
            total = total + chain[table[j, 3, k]]
        return total

    def sib_copy(d):
        return pltpu.make_async_remote_copy(
            src_ref=sib_send.at[d],
            dst_ref=sib_recv.at[d],
            send_sem=sib_send_sem.at[d],
            recv_sem=sib_recv_sem.at[d],
            device_id=sibling,
            device_id_type=MESH,
        )

    lower = place < line // 2

    def gather(i, carry):
        d = jnp.where(lower, line - 1 - i, i)
        for g in range(group):
            sib_send[d, g * BS:(g + 1) * BS] = block_sum((2 * d + 1 - core) * group + g)
        sib_copy(d).start()
        for g in range(group):
            own[d, g * BS:(g + 1) * BS] = block_sum((2 * d + core) * group + g)
        return carry

    lax.fori_loop(0, line, gather, 0)

    def rows_of(g):
        return pl.ds(0, PAD + BS) if g == 0 else pl.ds(PAD + g * BS, BS)

    def up_copy(d, g):
        return pltpu.make_async_remote_copy(
            src_ref=box_send.at[d, rows_of(g)],
            dst_ref=up_recv.at[d, rows_of(g)],
            send_sem=box_send_sem.at[d, g],
            recv_sem=up_sem.at[d, g],
            device_id=above,
            device_id_type=MESH,
        )

    def down_copy(d, g):
        return pltpu.make_async_remote_copy(
            src_ref=box_send.at[d, rows_of(g)],
            dst_ref=down_recv.at[d, rows_of(g)],
            send_sem=box_send_sem.at[d, g],
            recv_sem=down_sem.at[d, g],
            device_id=below,
            device_id_type=MESH,
        )

    def hop(d, copy, box, first):
        sib_copy(d).wait_recv()
        both = own[d] + sib_recv[d]
        own[d] = both
        top = jnp.max(jnp.abs(both), axis=0, keepdims=True)
        if not first:
            copy(d, 0).wait_recv()
            scale = scale_of(read_code(box.at[d]))
            top = top + scale
        code = jnp.ceil(jnp.log2(jnp.maximum(top, TINY)) * STEPS)
        inverse = 1.0 / scale_of(code)
        box_send[d, 0:PAD] = (
            jnp.broadcast_to(code, (PAD, width)).astype(jnp.int32).astype(jnp.int16)
        )
        for g in range(group):
            total = own[d, g * BS:(g + 1) * BS]
            if not first:
                if g:
                    copy(d, g).wait_recv()
                total = total + decode(box.at[d], g, scale)
            whole = jnp.round(total * inverse * LEVELS).astype(jnp.int32)
            box_send[d, PAD + g * BS:PAD + (g + 1) * BS] = whole.astype(jnp.int16)
            copy(d, g).start()

    def step(s, carry):
        up_to = line - 1 - s + place
        down_to = s - (line - 1) + place

        @pl.when(jnp.logical_and(place <= s, place == 0))
        def _():
            hop(up_to, up_copy, up_recv, True)

        @pl.when(jnp.logical_and(place <= s, place > 0))
        def _():
            hop(up_to, up_copy, up_recv, False)

        @pl.when(jnp.logical_and(line - 1 - place <= s, place == line - 1))
        def _():
            hop(down_to, down_copy, down_recv, True)

        @pl.when(jnp.logical_and(line - 1 - place <= s, place < line - 1))
        def _():
            hop(down_to, down_copy, down_recv, False)

        return carry

    lax.fori_loop(0, line - 1, step, 0)

    sib_copy(place).wait_recv()
    own[place] = own[place] + sib_recv[place]
    w = w_ref[...]
    for g in range(group):
        block = pl.ds(g * BS, BS)

        @pl.when(place > 0)
        def _():
            up_copy(place, g).wait_recv()
            scale = scale_of(read_code(up_recv.at[place]))
            own[place, block] = own[place, block] + decode(up_recv.at[place], g, scale)

        @pl.when(place < line - 1)
        def _():
            down_copy(place, g).wait_recv()
            scale = scale_of(read_code(down_recv.at[place]))
            own[place, block] = own[place, block] + decode(down_recv.at[place], g, scale)

        total = own[place, block]
        high = total.astype(jnp.bfloat16)
        low = (total - high.astype(jnp.float32)).astype(jnp.bfloat16)
        result = jnp.dot(high, w, preferred_element_type=jnp.float32) + jnp.dot(
            low, w, preferred_element_type=jnp.float32
        )
        out_ref[block] = jnp.maximum(result, 0.0).astype(jnp.bfloat16)

    for send in sends:
        send.wait_send()

    def finish(d, carry):
        sib_copy(d).wait_send()

        @pl.when(d > place)
        def _():
            for g in range(group):
                up_copy(d, g).wait_send()

        @pl.when(d < place)
        def _():
            for g in range(group):
                down_copy(d, g).wait_send()

        return carry

    lax.fori_loop(0, line, finish, 0)


def local(node_feats, block_vals, block_rows, block_cols, block_count, weight):
    n_blk = lax.axis_size("blk")
    line = lax.axis_size("rep") // 2
    width = node_feats.shape[1]
    x = node_feats.reshape(-1, BS, width)
    group = x.shape[0]
    vals = block_vals[0, 0]
    rows = block_rows[0, 0]
    cols = block_cols[0, 0]
    count = block_count[0]
    slots = rows.shape[1]
    unit = group * BS
    vmem = pl.BlockSpec(memory_space=pltpu.VMEM)
    anywhere = pl.BlockSpec(memory_space=pl.ANY)
    dma = pltpu.SemaphoreType.DMA
    return pl.pallas_call(
        functools.partial(kernel, n_blk, line, group),
        out_shape=jax.ShapeDtypeStruct((unit, weight.shape[1]), jnp.bfloat16),
        in_specs=[anywhere] * 6,
        out_specs=vmem,
        scratch_shapes=[
            pltpu.VMEM(rows.shape, jnp.int32),
            pltpu.VMEM(cols.shape, jnp.int32),
            pltpu.VMEM(count.shape, jnp.int32),
            pltpu.VMEM(weight.shape, jnp.bfloat16),
            pltpu.VMEM((n_blk, 8, 128), jnp.int32),
            pltpu.SMEM((n_blk, 8, 128), jnp.int32),
            pltpu.VMEM((n_blk * slots + 1, BS, width), jnp.float32),
            pltpu.VMEM((line, unit, width), jnp.float32),
            pltpu.VMEM((line, unit, width), jnp.float32),
            pltpu.VMEM((line, unit, width), jnp.float32),
            pltpu.VMEM((line, unit + PAD, width), jnp.int16),
            pltpu.VMEM((line, unit + PAD, width), jnp.int16),
            pltpu.VMEM((line, unit + PAD, width), jnp.int16),
            dma((n_blk,)), dma((n_blk, 2)), dma((n_blk, 2)),
            dma((line,)), dma((line,)),
            dma((line, group)), dma((line, group)), dma((line, group)),
            dma, dma((5,)),
        ]
        + [pltpu.VMEM((group, BS, width), jnp.bfloat16)] * n_blk
        + [pltpu.VMEM(vals.shape[1:], jnp.bfloat16)] * n_blk,
        compiler_params=pltpu.CompilerParams(
            collective_id=0, has_side_effects=True, vmem_limit_bytes=56 * 1024 * 1024
        ),
        cost_estimate=pl.CostEstimate(
            flops=2 * n_blk * slots * BS * BS * width,
            bytes_accessed=2 * n_blk * slots * BS * BS,
            transcendentals=0,
        ),
    )(x, vals, rows, cols, count, weight)


def solution(mesh):
    return jax.shard_map(
        local,
        mesh=mesh,
        in_specs=(
            P(("blk", "rep"), None),
            P("blk", "rep", None, None, None, None),
            P("blk", "rep", None, None),
            P("blk", "rep", None, None),
            P("blk", "rep", None),
            P(),
        ),
        out_specs=P(("blk", "rep"), None),
        check_vma=False,
    )
```

```python
import functools

import jax
import jax.numpy as jnp
from jax import lax
from jax.experimental import pallas as pl
from jax.experimental.pallas import tpu as pltpu
from jax.sharding import PartitionSpec as P

BS = 128
LEVELS = 32000.0
STEPS = 256.0
TINY = 1e-36
PAD = 16
MESH = pl.DeviceIdType.MESH


def flip(index, mask, size):
    if size & (size - 1):
        return (index + mask) % size
    out = index
    bit = 1
    while bit < size:
        if mask & bit:
            out = out + bit * (1 - 2 * ((index // bit) % 2))
        bit *= 2
    return out


def back(mask, size):
    return (size - mask) % size if size & (size - 1) else mask


def scale_of(code):
    return jnp.exp2(code * (1.0 / STEPS))


def read_code(box):
    return box[pl.ds(0, PAD)].astype(jnp.int32).astype(jnp.float32)[0:1]


def decode(box, g, scale):
    part = box[pl.ds(PAD + g * BS, BS)].astype(jnp.int32).astype(jnp.float32)
    return part * (1.0 / LEVELS) * scale


def prepare(rows, cols, live_count, prep, base, nothing, panel, group):
    slots = rows.shape[1]
    lane = lax.broadcasted_iota(jnp.int32, (slots, slots), 1)
    sub = lax.broadcasted_iota(jnp.int32, (slots, slots), 0)
    place = lax.broadcasted_iota(jnp.int32, (slots, panel), 1)
    col_bits = max(1, (group - 1).bit_length())
    slot_bits = max(1, (slots - 1).bit_length())
    row_bits = col_bits + slot_bits

    live = lane[0:1] < live_count
    key = jnp.where(live, rows, panel)
    col = jnp.where(live, cols, 0)
    word = key * (1 << row_bits) + lane[0:1] * (1 << col_bits) + col
    spread = jnp.broadcast_to(word, (slots, slots))
    word_up = jnp.sum(jnp.where(lane == sub, spread, 0), axis=1, keepdims=True)
    rank = jnp.sum(jnp.where(word < word_up, 1, 0), axis=1, keepdims=True)
    key_up = word_up >> row_bits
    before = jnp.max(jnp.where(rank == lane - 1, key_up, -1), axis=0, keepdims=True)
    ordered = jnp.sum(jnp.where(rank == lane, word_up, 0), axis=0, keepdims=True)
    prep[0:1, 0:slots] = (ordered >> col_bits) & ((1 << slot_bits) - 1)
    prep[1:2, 0:slots] = ordered & ((1 << col_bits) - 1)
    prep[2:3, 0:slots] = jnp.where(before == (ordered >> row_bits), 1, 0)
    upto = jnp.sum(jnp.where(key_up <= place, 1, 0), axis=0, keepdims=True)
    found = jnp.max(jnp.where(key_up == place, 1, 0), axis=0, keepdims=True)
    prep[3:4, 0:panel] = jnp.where(found > 0, upto + (base - 1), nothing)


def kernel(
    n_blk, line, group,
    x_hbm, vals_hbm, rows_hbm, cols_hbm, count_hbm, w_hbm, out_ref,
    rows_ref, cols_ref, count_ref, w_ref, prep, table, chain, own, sib_send, sib_recv, box_send, up_recv, down_recv,
    vals_sem, x_send_sem, x_recv_sem, sib_send_sem, sib_recv_sem,
    box_send_sem, up_sem, down_sem, table_sem, in_sem, *pieces_and_vals,
):
    pieces = pieces_and_vals[:n_blk]
    vals = pieces_and_vals[n_blk:]
    slots = vals_hbm.shape[1]
    width = x_hbm.shape[2]
    blk = lax.axis_index("blk")
    rep = lax.axis_index("rep")
    place = rep // 2
    core = rep % 2
    sibling = {"rep": place * 2 + 1 - core}
    above = {"rep": rep + 2}
    below = {"rep": rep - 2}

    square = n_blk == 4
    direct = (1, 2) if square else tuple(range(1, n_blk))

    barrier = pltpu.get_barrier_semaphore()
    for turn in direct:
        pl.semaphore_signal(
            barrier, inc=1, device_id={"blk": flip(blk, turn, n_blk)}, device_id_type=MESH
        )
    pl.semaphore_signal(barrier, inc=1, device_id=sibling, device_id_type=MESH)

    @pl.when(place < line - 1)
    def _():
        pl.semaphore_signal(barrier, inc=1, device_id=above, device_id_type=MESH)

    @pl.when(place > 0)
    def _():
        pl.semaphore_signal(barrier, inc=1, device_id=below, device_id_type=MESH)

    fetches = [
        pltpu.make_async_copy(source, target, in_sem.at[i])
        for i, (source, target) in enumerate((
            (rows_hbm, rows_ref),
            (cols_hbm, cols_ref),
            (count_hbm, count_ref),
            (x_hbm, pieces[0]),
            (w_hbm, w_ref),
        ))
    ]
    for fetch in fetches:
        fetch.start()

    def load(turn):
        j = flip(blk, back(turn, n_blk), n_blk)
        return pltpu.make_async_copy(vals_hbm.at[j], vals[turn], vals_sem.at[turn])

    load(0).start()

    peers = len(direct) + 1 + jnp.where(place > 0, 1, 0) + jnp.where(place < line - 1, 1, 0)
    pl.semaphore_wait(barrier, peers)

    def half(ref, h):
        return ref.at[:, pl.ds(h * (BS // 2), BS // 2)]

    def pass_on(source, turn, h, to):
        return pltpu.make_async_remote_copy(
            src_ref=half(source, h),
            dst_ref=half(pieces[turn], h),
            send_sem=x_send_sem.at[turn, h],
            recv_sem=x_recv_sem.at[turn, h],
            device_id={"blk": flip(blk, to, n_blk)},
            device_id_type=MESH,
        )

    sends = [
        pass_on(x_hbm, turn, (first + turn + 1) % 2, turn) for first in (0, 1) for turn in direct
    ]
    for send in sends:
        send.start()
    for turn in range(1, n_blk):
        load(turn).start()

    prep[...] = jnp.zeros(prep.shape, jnp.int32)
    for fetch in fetches[:3]:
        fetch.wait()

    def index(turn):
        j = flip(blk, back(turn, n_blk), n_blk)
        prepare(
            rows_ref[pl.ds(j, 1), :], cols_ref[pl.ds(j, 1), :], count_ref[0, j],
            prep.at[turn], turn * slots, n_blk * slots, group * 2 * line, group,
        )

    fills = [
        pltpu.make_async_copy(prep.at[turn], table.at[turn], table_sem.at[turn])
        for turn in range(n_blk)
    ]
    index(0)
    fills[0].start()
    chain[n_blk * slots] = jnp.zeros((BS, width), jnp.float32)

    fills[0].wait()
    for fetch in fetches[3:]:
        fetch.wait()
    batch = max(u for u in range(1, 41) if slots % u == 0)
    for turn in range(n_blk):
        if square and turn == 1:
            for near, h in ((1, 0), (2, 1)):
                pass_on(x_hbm, near, h, near).wait_recv()
                onward = pass_on(pieces[near], 3, h, 3 - near)
                onward.start()
                sends.append(onward)
        load(turn).wait()
        for h in (0, 1) if turn else ():
            if not (square and h == turn - 1):
                pass_on(x_hbm, turn, h, direct[0]).wait_recv()

        if turn:
            fills[turn].wait()

        def some(g, total, j=turn, piece=pieces[turn], blocks=vals[turn]):
            for u in range(batch):
                t = g * batch + u
                product = jnp.dot(
                    blocks[table[j, 0, t]],
                    piece[table[j, 1, t]],
                    preferred_element_type=jnp.float32,
                )
                total = total * table[j, 2, t].astype(jnp.float32) + product
                chain[j * slots + t] = total
            return total

        if turn == 0:
            for later in range(1, n_blk):
                index(later)
        total = jnp.zeros((BS, width), jnp.float32)
        if slots == batch:
            some(0, total)
        else:
            lax.fori_loop(0, slots // batch, some, total)
        if turn == 0:
            for later in range(1, n_blk):
                fills[later].start()

    def block_sum(k):
        total = chain[table[0, 3, k]]
        for j in range(1, n_blk):
            total = total + chain[table[j, 3, k]]
        return total

    def sib_copy(d):
        return pltpu.make_async_remote_copy(
            src_ref=sib_send.at[d],
            dst_ref=sib_recv.at[d],
            send_sem=sib_send_sem.at[d],
            recv_sem=sib_recv_sem.at[d],
            device_id=sibling,
            device_id_type=MESH,
        )

    lower = place < line // 2

    def gather(i, carry):
        d = jnp.where(lower, line - 1 - i, i)
        for g in range(group):
            sib_send[d, g * BS:(g + 1) * BS] = block_sum((2 * d + 1 - core) * group + g)
        sib_copy(d).start()
        for g in range(group):
            own[d, g * BS:(g + 1) * BS] = block_sum((2 * d + core) * group + g)
        return carry

    lax.fori_loop(0, line, gather, 0)

    def rows_of(g):
        return pl.ds(0, PAD + BS) if g == 0 else pl.ds(PAD + g * BS, BS)

    def up_copy(d, g):
        return pltpu.make_async_remote_copy(
            src_ref=box_send.at[d, rows_of(g)],
            dst_ref=up_recv.at[d, rows_of(g)],
            send_sem=box_send_sem.at[d, g],
            recv_sem=up_sem.at[d, g],
            device_id=above,
            device_id_type=MESH,
        )

    def down_copy(d, g):
        return pltpu.make_async_remote_copy(
            src_ref=box_send.at[d, rows_of(g)],
            dst_ref=down_recv.at[d, rows_of(g)],
            send_sem=box_send_sem.at[d, g],
            recv_sem=down_sem.at[d, g],
            device_id=below,
            device_id_type=MESH,
        )

    def hop(d, copy, box, first):
        sib_copy(d).wait_recv()
        both = own[d] + sib_recv[d]
        own[d] = both
        top = jnp.max(jnp.abs(both), axis=0, keepdims=True)
        if not first:
            copy(d, 0).wait_recv()
            scale = scale_of(read_code(box.at[d]))
            top = top + scale
        code = jnp.ceil(jnp.log2(jnp.maximum(top, TINY)) * STEPS)
        inverse = 1.0 / scale_of(code)
        box_send[d, 0:PAD] = (
            jnp.broadcast_to(code, (PAD, width)).astype(jnp.int32).astype(jnp.int16)
        )
        for g in range(group):
            total = own[d, g * BS:(g + 1) * BS]
            if not first:
                if g:
                    copy(d, g).wait_recv()
                total = total + decode(box.at[d], g, scale)
            whole = jnp.round(total * inverse * LEVELS).astype(jnp.int32)
            box_send[d, PAD + g * BS:PAD + (g + 1) * BS] = whole.astype(jnp.int16)
            copy(d, g).start()

    def step(s, carry):
        up_to = line - 1 - s + place
        down_to = s - (line - 1) + place

        @pl.when(jnp.logical_and(place <= s, place == 0))
        def _():
            hop(up_to, up_copy, up_recv, True)

        @pl.when(jnp.logical_and(place <= s, place > 0))
        def _():
            hop(up_to, up_copy, up_recv, False)

        @pl.when(jnp.logical_and(line - 1 - place <= s, place == line - 1))
        def _():
            hop(down_to, down_copy, down_recv, True)

        @pl.when(jnp.logical_and(line - 1 - place <= s, place < line - 1))
        def _():
            hop(down_to, down_copy, down_recv, False)

        return carry

    lax.fori_loop(0, line - 1, step, 0)

    sib_copy(place).wait_recv()
    own[place] = own[place] + sib_recv[place]
    w = w_ref[...]
    for g in range(group):
        block = pl.ds(g * BS, BS)

        @pl.when(place > 0)
        def _():
            up_copy(place, g).wait_recv()
            scale = scale_of(read_code(up_recv.at[place]))
            own[place, block] = own[place, block] + decode(up_recv.at[place], g, scale)

        @pl.when(place < line - 1)
        def _():
            down_copy(place, g).wait_recv()
            scale = scale_of(read_code(down_recv.at[place]))
            own[place, block] = own[place, block] + decode(down_recv.at[place], g, scale)

        total = own[place, block]
        high = total.astype(jnp.bfloat16)
        low = (total - high.astype(jnp.float32)).astype(jnp.bfloat16)
        result = jnp.dot(high, w, preferred_element_type=jnp.float32) + jnp.dot(
            low, w, preferred_element_type=jnp.float32
        )
        out_ref[block] = jnp.maximum(result, 0.0).astype(jnp.bfloat16)

    for send in sends:
        send.wait_send()

    def finish(d, carry):
        sib_copy(d).wait_send()

        @pl.when(d > place)
        def _():
            for g in range(group):
                up_copy(d, g).wait_send()

        @pl.when(d < place)
        def _():
            for g in range(group):
                down_copy(d, g).wait_send()

        return carry

    lax.fori_loop(0, line, finish, 0)


def local(node_feats, block_vals, block_rows, block_cols, block_count, weight):
    n_blk = lax.axis_size("blk")
    line = lax.axis_size("rep") // 2
    width = node_feats.shape[1]
    x = node_feats.reshape(-1, BS, width)
    group = x.shape[0]
    vals = block_vals[0, 0]
    rows = block_rows[0, 0]
    cols = block_cols[0, 0]
    count = block_count[0]
    slots = rows.shape[1]
    unit = group * BS
    vmem = pl.BlockSpec(memory_space=pltpu.VMEM)
    anywhere = pl.BlockSpec(memory_space=pl.ANY)
    dma = pltpu.SemaphoreType.DMA
    return pl.pallas_call(
        functools.partial(kernel, n_blk, line, group),
        out_shape=jax.ShapeDtypeStruct((unit, weight.shape[1]), jnp.bfloat16),
        in_specs=[anywhere] * 6,
        out_specs=vmem,
        scratch_shapes=[
            pltpu.VMEM(rows.shape, jnp.int32),
            pltpu.VMEM(cols.shape, jnp.int32),
            pltpu.SMEM(count.shape, jnp.int32),
            pltpu.VMEM(weight.shape, jnp.bfloat16),
            pltpu.VMEM((n_blk, 8, 128), jnp.int32),
            pltpu.SMEM((n_blk, 8, 128), jnp.int32),
            pltpu.VMEM((n_blk * slots + 1, BS, width), jnp.float32),
            pltpu.VMEM((line, unit, width), jnp.float32),
            pltpu.VMEM((line, unit, width), jnp.float32),
            pltpu.VMEM((line, unit, width), jnp.float32),
            pltpu.VMEM((line, unit + PAD, width), jnp.int16),
            pltpu.VMEM((line, unit + PAD, width), jnp.int16),
            pltpu.VMEM((line, unit + PAD, width), jnp.int16),
            dma((n_blk,)), dma((n_blk, 2)), dma((n_blk, 2)),
            dma((line,)), dma((line,)),
            dma((line, group)), dma((line, group)), dma((line, group)),
            dma((n_blk,)), dma((5,)),
        ]
        + [pltpu.VMEM((group, BS, width), jnp.bfloat16)] * n_blk
        + [pltpu.VMEM(vals.shape[1:], jnp.bfloat16)] * n_blk,
        compiler_params=pltpu.CompilerParams(
            collective_id=0, has_side_effects=True, vmem_limit_bytes=56 * 1024 * 1024
        ),
        cost_estimate=pl.CostEstimate(
            flops=2 * n_blk * slots * BS * BS * width,
            bytes_accessed=2 * n_blk * slots * BS * BS,
            transcendentals=0,
        ),
    )(x, vals, rows, cols, count, weight)


def solution(mesh):
    return jax.shard_map(
        local,
        mesh=mesh,
        in_specs=(
            P(("blk", "rep"), None),
            P("blk", "rep", None, None, None, None),
            P("blk", "rep", None, None),
            P("blk", "rep", None, None),
            P("blk", "rep", None),
            P(),
        ),
        out_specs=P(("blk", "rep"), None),
        check_vma=False,
    )
```

```python
import functools
import math

import jax
import jax.numpy as jnp
from jax import lax
from jax.experimental import pallas as pl
from jax.experimental.pallas import tpu as pltpu
from jax.sharding import PartitionSpec as P

BS = 128
LEVELS = 32000.0
STEPS = 256.0
TINY = 1e-36
PAD = 16
MESH = pl.DeviceIdType.MESH


def flip(index, mask, size):
    if size & (size - 1):
        return (index + mask) % size
    out = index
    bit = 1
    while bit < size:
        if mask & bit:
            out = out + bit * (1 - 2 * ((index // bit) % 2))
        bit *= 2
    return out


def back(mask, size):
    return (size - mask) % size if size & (size - 1) else mask


def scale_of(code):
    return jnp.exp2(code * (1.0 / STEPS))


def read_code(box):
    return box[pl.ds(0, PAD)].astype(jnp.int32).astype(jnp.float32)[0:1]


def decode(box, g, scale):
    part = box[pl.ds(PAD + g * BS, BS)].astype(jnp.int32).astype(jnp.float32)
    return part * (1.0 / LEVELS) * scale


def prepare(rows, cols, live_count, prep, base, nothing, panel, group):
    slots = rows.shape[1]
    lane = lax.broadcasted_iota(jnp.int32, (slots, slots), 1)
    sub = lax.broadcasted_iota(jnp.int32, (slots, slots), 0)
    place = lax.broadcasted_iota(jnp.int32, (slots, panel), 1)
    col_bits = max(1, (group - 1).bit_length())
    slot_bits = max(1, (slots - 1).bit_length())
    row_bits = col_bits + slot_bits

    live = lane[0:1] < live_count
    key = jnp.where(live, rows, panel)
    col = jnp.where(live, cols, 0)
    word = key * (1 << row_bits) + lane[0:1] * (1 << col_bits) + col
    spread = jnp.broadcast_to(word, (slots, slots))
    word_up = jnp.sum(jnp.where(lane == sub, spread, 0), axis=1, keepdims=True)
    rank = jnp.sum(jnp.where(word < word_up, 1, 0), axis=1, keepdims=True)
    key_up = word_up >> row_bits
    before = jnp.max(jnp.where(rank == lane - 1, key_up, -1), axis=0, keepdims=True)
    ordered = jnp.sum(jnp.where(rank == lane, word_up, 0), axis=0, keepdims=True)
    prep[0:1, 0:slots] = (ordered >> col_bits) & ((1 << slot_bits) - 1)
    prep[1:2, 0:slots] = ordered & ((1 << col_bits) - 1)
    prep[2:3, 0:slots] = jnp.where(before == (ordered >> row_bits), 1, 0)
    upto = jnp.sum(jnp.where(key_up <= place, 1, 0), axis=0, keepdims=True)
    found = jnp.max(jnp.where(key_up == place, 1, 0), axis=0, keepdims=True)
    prep[3:4, 0:panel] = jnp.where(found > 0, upto + (base - 1), nothing)


def kernel(
    n_blk, line, group,
    x_hbm, vals_hbm, rows_hbm, cols_hbm, count_hbm, w_hbm, out_ref,
    rows_ref, cols_ref, count_ref, w_ref, prep, table, chain, own, sib_send, sib_recv, box_send, up_recv, down_recv,
    vals_sem, x_send_sem, x_recv_sem, sib_send_sem, sib_recv_sem,
    box_send_sem, up_sem, down_sem, table_sem, in_sem, *pieces_and_vals,
):
    pieces = pieces_and_vals[:n_blk]
    vals = pieces_and_vals[n_blk:]
    slots = vals_hbm.shape[1]
    width = x_hbm.shape[2]
    blk = lax.axis_index("blk")
    rep = lax.axis_index("rep")
    place = rep // 2
    core = rep % 2
    sibling = {"rep": place * 2 + 1 - core}
    above = {"rep": rep + 2}
    below = {"rep": rep - 2}

    square = n_blk == 4
    direct = (1, 2) if square else tuple(range(1, n_blk))

    barrier = pltpu.get_barrier_semaphore()
    for turn in direct:
        pl.semaphore_signal(
            barrier, inc=1, device_id={"blk": flip(blk, turn, n_blk)}, device_id_type=MESH
        )
    pl.semaphore_signal(barrier, inc=1, device_id=sibling, device_id_type=MESH)

    @pl.when(place < line - 1)
    def _():
        pl.semaphore_signal(barrier, inc=1, device_id=above, device_id_type=MESH)

    @pl.when(place > 0)
    def _():
        pl.semaphore_signal(barrier, inc=1, device_id=below, device_id_type=MESH)

    fetches = [
        pltpu.make_async_copy(source, target, in_sem.at[i])
        for i, (source, target) in enumerate((
            (rows_hbm, rows_ref),
            (cols_hbm, cols_ref),
            (count_hbm, count_ref),
            (x_hbm, pieces[0]),
            (w_hbm, w_ref),
        ))
    ]
    for fetch in fetches:
        fetch.start()

    def load(turn):
        j = flip(blk, back(turn, n_blk), n_blk)
        return pltpu.make_async_copy(vals_hbm.at[j], vals[turn], vals_sem.at[turn])

    load(0).start()

    peers = len(direct) + 1 + jnp.where(place > 0, 1, 0) + jnp.where(place < line - 1, 1, 0)
    pl.semaphore_wait(barrier, peers)

    def half(ref, h):
        return ref.at[:, pl.ds(h * (BS // 2), BS // 2)]

    def pass_on(source, turn, h, to):
        return pltpu.make_async_remote_copy(
            src_ref=half(source, h),
            dst_ref=half(pieces[turn], h),
            send_sem=x_send_sem.at[turn, h],
            recv_sem=x_recv_sem.at[turn, h],
            device_id={"blk": flip(blk, to, n_blk)},
            device_id_type=MESH,
        )

    sends = [
        pass_on(x_hbm, turn, (first + turn + 1) % 2, turn) for first in (0, 1) for turn in direct
    ]
    for send in sends:
        send.start()
    for turn in range(1, n_blk):
        load(turn).start()

    prep[...] = jnp.zeros(prep.shape, jnp.int32)
    for fetch in fetches[:3]:
        fetch.wait()

    def index(turn):
        j = flip(blk, back(turn, n_blk), n_blk)
        prepare(
            rows_ref[pl.ds(j, 1), :], cols_ref[pl.ds(j, 1), :], count_ref[0, j],
            prep.at[turn], turn * slots, n_blk * slots, group * 2 * line, group,
        )

    fills = [
        pltpu.make_async_copy(prep.at[turn], table.at[turn], table_sem.at[turn])
        for turn in range(n_blk)
    ]
    index(0)
    fills[0].start()
    chain[n_blk * slots] = jnp.zeros((BS, width), jnp.float32)

    fills[0].wait()
    for fetch in fetches[3:]:
        fetch.wait()
    batch = max(u for u in range(1, 41) if slots % u == 0)
    lower = place < line // 2

    def early_sum(k):
        total = chain[table[0, 3, k]]
        for turn in range(1, n_blk - 1):
            total = total + chain[table[turn, 3, k]]
        return total

    def last_sum(k):
        return chain[table[n_blk - 1, 3, k]]

    def early(d, carry):
        for g in range(group):
            at = (d, pl.ds(g * BS, BS))
            sib_send[at] = early_sum((2 * d + 1 - core) * group + g)
            own[at] = early_sum((2 * d + core) * group + g)
        return carry

    for turn in range(n_blk):
        if turn == n_blk - 1:
            lax.fori_loop(0, line, early, 0)
        if square and turn == 1:
            for near, h in ((1, 0), (2, 1)):
                pass_on(x_hbm, near, h, near).wait_recv()
                onward = pass_on(pieces[near], 3, h, 3 - near)
                onward.start()
                sends.append(onward)
        load(turn).wait()
        for h in (0, 1) if turn else ():
            if not (square and h == turn - 1):
                pass_on(x_hbm, turn, h, direct[0]).wait_recv()

        if turn:
            fills[turn].wait()

        def some(g, total, j=turn, piece=pieces[turn], blocks=vals[turn]):
            for u in range(batch):
                t = g * batch + u
                product = jnp.dot(
                    blocks[table[j, 0, t]],
                    piece[table[j, 1, t]],
                    preferred_element_type=jnp.float32,
                )
                total = total * table[j, 2, t].astype(jnp.float32) + product
                chain[j * slots + t] = total
            return total

        if turn == 0:
            for later in range(1, n_blk):
                index(later)
        total = jnp.zeros((BS, width), jnp.float32)
        if slots == batch:
            some(0, total)
        else:
            lax.fori_loop(0, slots // batch, some, total)
        if turn == 0:
            for later in range(1, n_blk):
                fills[later].start()

    def sib_copy(d):
        return pltpu.make_async_remote_copy(
            src_ref=sib_send.at[d],
            dst_ref=sib_recv.at[d],
            send_sem=sib_send_sem.at[d],
            recv_sem=sib_recv_sem.at[d],
            device_id=sibling,
            device_id_type=MESH,
        )

    def gather(i, carry):
        d = jnp.where(lower, line - 1 - i, i)
        for g in range(group):
            at = (d, pl.ds(g * BS, BS))
            sib_send[at] = sib_send[at] + last_sum((2 * d + 1 - core) * group + g)
        sib_copy(d).start()
        for g in range(group):
            at = (d, pl.ds(g * BS, BS))
            own[at] = own[at] + last_sum((2 * d + core) * group + g)
        return carry

    lax.fori_loop(0, line, gather, 0)

    def rows_of(g):
        return pl.ds(0, PAD + BS) if g == 0 else pl.ds(PAD + g * BS, BS)

    def up_copy(d, g):
        return pltpu.make_async_remote_copy(
            src_ref=box_send.at[d, rows_of(g)],
            dst_ref=up_recv.at[d, rows_of(g)],
            send_sem=box_send_sem.at[d, g],
            recv_sem=up_sem.at[d, g],
            device_id=above,
            device_id_type=MESH,
        )

    def down_copy(d, g):
        return pltpu.make_async_remote_copy(
            src_ref=box_send.at[d, rows_of(g)],
            dst_ref=down_recv.at[d, rows_of(g)],
            send_sem=box_send_sem.at[d, g],
            recv_sem=down_sem.at[d, g],
            device_id=below,
            device_id_type=MESH,
        )

    def hop(d, copy, box, first):
        sib_copy(d).wait_recv()
        both = own[d] + sib_recv[d]
        own[d] = both
        top = jnp.max(jnp.abs(both), axis=0, keepdims=True)
        if not first:
            copy(d, 0).wait_recv()
            scale = scale_of(read_code(box.at[d]))
            top = top + scale
        code = jnp.ceil(jnp.log2(jnp.maximum(top, TINY)) * STEPS)
        inverse = 1.0 / scale_of(code)
        box_send[d, 0:PAD] = (
            jnp.broadcast_to(code, (PAD, width)).astype(jnp.int32).astype(jnp.int16)
        )
        for g in range(group):
            total = own[d, g * BS:(g + 1) * BS]
            if not first:
                if g:
                    copy(d, g).wait_recv()
                total = total + decode(box.at[d], g, scale)
            whole = jnp.round(total * inverse * LEVELS).astype(jnp.int32)
            box_send[d, PAD + g * BS:PAD + (g + 1) * BS] = whole.astype(jnp.int16)
            copy(d, g).start()

    def step(s, carry):
        up_to = line - 1 - s + place
        down_to = s - (line - 1) + place

        @pl.when(jnp.logical_and(place <= s, place == 0))
        def _():
            hop(up_to, up_copy, up_recv, True)

        @pl.when(jnp.logical_and(place <= s, place > 0))
        def _():
            hop(up_to, up_copy, up_recv, False)

        @pl.when(jnp.logical_and(line - 1 - place <= s, place == line - 1))
        def _():
            hop(down_to, down_copy, down_recv, True)

        @pl.when(jnp.logical_and(line - 1 - place <= s, place < line - 1))
        def _():
            hop(down_to, down_copy, down_recv, False)

        return carry

    lax.fori_loop(0, line - 1, step, 0)

    sib_copy(place).wait_recv()
    own[place] = own[place] + sib_recv[place]
    w = w_ref[...]
    for g in range(group):
        block = pl.ds(g * BS, BS)

        @pl.when(place > 0)
        def _():
            up_copy(place, g).wait_recv()
            scale = scale_of(read_code(up_recv.at[place]))
            own[place, block] = own[place, block] + decode(up_recv.at[place], g, scale)

        @pl.when(place < line - 1)
        def _():
            down_copy(place, g).wait_recv()
            scale = scale_of(read_code(down_recv.at[place]))
            own[place, block] = own[place, block] + decode(down_recv.at[place], g, scale)

        total = own[place, block]
        high = total.astype(jnp.bfloat16)
        low = (total - high.astype(jnp.float32)).astype(jnp.bfloat16)
        result = jnp.dot(high, w, preferred_element_type=jnp.float32) + jnp.dot(
            low, w, preferred_element_type=jnp.float32
        )
        out_ref[block] = jnp.maximum(result, 0.0).astype(jnp.bfloat16)

    for send in sends:
        send.wait_send()

    def finish(d, carry):
        sib_copy(d).wait_send()

        @pl.when(d > place)
        def _():
            for g in range(group):
                up_copy(d, g).wait_send()

        @pl.when(d < place)
        def _():
            for g in range(group):
                down_copy(d, g).wait_send()

        return carry

    lax.fori_loop(0, line, finish, 0)


def local(node_feats, block_vals, block_rows, block_cols, block_count, weight):
    n_blk = lax.axis_size("blk")
    line = lax.axis_size("rep") // 2
    width = node_feats.shape[1]
    x = node_feats.reshape(-1, BS, width)
    group = x.shape[0]
    vals = block_vals[0, 0]
    rows = block_rows[0, 0]
    cols = block_cols[0, 0]
    count = block_count[0]
    slots = rows.shape[1]
    unit = group * BS
    vmem = pl.BlockSpec(memory_space=pltpu.VMEM)
    far = pl.BlockSpec(memory_space=pltpu.HBM)
    operands = (x, vals, rows, cols, count, weight)
    dma = pltpu.SemaphoreType.DMA
    scratch = [
        pltpu.VMEM(rows.shape, jnp.int32),
        pltpu.VMEM(cols.shape, jnp.int32),
        pltpu.SMEM(count.shape, jnp.int32),
        pltpu.VMEM(weight.shape, jnp.bfloat16),
        pltpu.VMEM((n_blk, 8, 128), jnp.int32),
        pltpu.SMEM((n_blk, 8, 128), jnp.int32),
        pltpu.VMEM((n_blk * slots + 1, BS, width), jnp.float32),
        pltpu.VMEM((line, unit, width), jnp.float32),
        pltpu.VMEM((line, unit, width), jnp.float32),
        pltpu.VMEM((line, unit, width), jnp.float32),
        pltpu.VMEM((line, unit + PAD, width), jnp.int16),
        pltpu.VMEM((line, unit + PAD, width), jnp.int16),
        pltpu.VMEM((line, unit + PAD, width), jnp.int16),
    ]
    semaphores = [
        dma((n_blk,)), dma((n_blk, 2)), dma((n_blk, 2)),
        dma((line,)), dma((line,)),
        dma((line, group)), dma((line, group)), dma((line, group)),
        dma((n_blk,)), dma((5,)),
    ]
    landing = [pltpu.VMEM((group, BS, width), jnp.bfloat16)] * n_blk
    landing += [pltpu.VMEM(vals.shape[1:], jnp.bfloat16)] * n_blk
    used = sum(
        math.prod(ref.shape) * jnp.dtype(ref.dtype).itemsize
        for ref in scratch + landing
    )
    return pl.pallas_call(
        functools.partial(kernel, n_blk, line, group),
        out_shape=jax.ShapeDtypeStruct((unit, weight.shape[1]), jnp.bfloat16),
        in_specs=[far] * 6,
        out_specs=vmem,
        scratch_shapes=scratch + semaphores + landing,
        compiler_params=pltpu.CompilerParams(
            collective_id=0, has_side_effects=True, vmem_limit_bytes=used + 4 * 1024 * 1024
        ),
        cost_estimate=pl.CostEstimate(
            flops=2 * n_blk * slots * BS * BS * width,
            bytes_accessed=2 * n_blk * slots * BS * BS,
            transcendentals=0,
        ),
    )(*(pltpu.with_memory_space_constraint(a, pltpu.HBM) for a in operands))


def solution(mesh):
    return jax.shard_map(
        local,
        mesh=mesh,
        in_specs=(
            P(("blk", "rep"), None),
            P("blk", "rep", None, None, None, None),
            P("blk", "rep", None, None),
            P("blk", "rep", None, None),
            P("blk", "rep", None),
            P(),
        ),
        out_specs=P(("blk", "rep"), None),
        check_vma=False,
    )
```

```python
import functools
import math

import jax
import jax.numpy as jnp
from jax import lax
from jax.experimental import pallas as pl
from jax.experimental.pallas import tpu as pltpu
from jax.sharding import PartitionSpec as P

BS = 128
LEVELS = 32000.0
STEPS = 256.0
TINY = 1e-36
PAD = 16
MESH = pl.DeviceIdType.MESH


def flip(index, mask, size):
    if size & (size - 1):
        return (index + mask) % size
    out = index
    bit = 1
    while bit < size:
        if mask & bit:
            out = out + bit * (1 - 2 * ((index // bit) % 2))
        bit *= 2
    return out


def back(mask, size):
    return (size - mask) % size if size & (size - 1) else mask


def scale_of(code):
    return jnp.exp2(code * (1.0 / STEPS))


def read_code(box):
    return box[pl.ds(0, PAD)].astype(jnp.int32).astype(jnp.float32)[0:1]


def decode(box, g, scale):
    part = box[pl.ds(PAD + g * BS, BS)].astype(jnp.int32).astype(jnp.float32)
    return part * (1.0 / LEVELS) * scale


def prepare(rows, cols, live_count, prep, base, nothing, panel, group):
    slots = rows.shape[1]
    lane = lax.broadcasted_iota(jnp.int32, (slots, slots), 1)
    sub = lax.broadcasted_iota(jnp.int32, (slots, slots), 0)
    place = lax.broadcasted_iota(jnp.int32, (slots, panel), 1)
    col_bits = max(1, (group - 1).bit_length())
    slot_bits = max(1, (slots - 1).bit_length())
    row_bits = col_bits + slot_bits

    live = lane[0:1] < live_count
    key = jnp.where(live, rows, panel)
    col = jnp.where(live, cols, 0)
    word = key * (1 << row_bits) + lane[0:1] * (1 << col_bits) + col
    spread = jnp.broadcast_to(word, (slots, slots))
    word_up = jnp.sum(jnp.where(lane == sub, spread, 0), axis=1, keepdims=True)
    rank = jnp.sum(jnp.where(word < word_up, 1, 0), axis=1, keepdims=True)
    key_up = word_up >> row_bits
    before = jnp.max(jnp.where(rank == lane - 1, key_up, -1), axis=0, keepdims=True)
    ordered = jnp.sum(jnp.where(rank == lane, word_up, 0), axis=0, keepdims=True)
    prep[0:1, 0:slots] = (ordered >> col_bits) & ((1 << slot_bits) - 1)
    prep[1:2, 0:slots] = ordered & ((1 << col_bits) - 1)
    prep[2:3, 0:slots] = jnp.where(before == (ordered >> row_bits), 1, 0)
    upto = jnp.sum(jnp.where(key_up <= place, 1, 0), axis=0, keepdims=True)
    found = jnp.max(jnp.where(key_up == place, 1, 0), axis=0, keepdims=True)
    prep[3:4, 0:panel] = jnp.where(found > 0, upto + (base - 1), nothing)


def kernel(
    n_blk, line, group,
    x_hbm, vals_hbm, rows_hbm, cols_hbm, count_hbm, w_hbm, out_ref,
    rows_ref, cols_ref, count_ref, w_ref, prep, table, chain, own, sib_send, sib_recv, box_send, up_recv, down_recv,
    vals_sem, x_send_sem, x_recv_sem, sib_send_sem, sib_recv_sem,
    box_send_sem, up_sem, down_sem, table_sem, in_sem, *pieces_and_vals,
):
    pieces = pieces_and_vals[:n_blk]
    vals = pieces_and_vals[n_blk:]
    slots = vals_hbm.shape[1]
    width = x_hbm.shape[2]
    blk = lax.axis_index("blk")
    rep = lax.axis_index("rep")
    place = rep // 2
    core = rep % 2
    sibling = {"rep": place * 2 + 1 - core}
    above = {"rep": rep + 2}
    below = {"rep": rep - 2}

    square = n_blk == 4
    direct = (1, 2) if square else tuple(range(1, n_blk))

    barrier = pltpu.get_barrier_semaphore()
    for turn in direct:
        pl.semaphore_signal(
            barrier, inc=1, device_id={"blk": flip(blk, turn, n_blk)}, device_id_type=MESH
        )
    pl.semaphore_signal(barrier, inc=1, device_id=sibling, device_id_type=MESH)

    @pl.when(place < line - 1)
    def _():
        pl.semaphore_signal(barrier, inc=1, device_id=above, device_id_type=MESH)

    @pl.when(place > 0)
    def _():
        pl.semaphore_signal(barrier, inc=1, device_id=below, device_id_type=MESH)

    fetches = [
        pltpu.make_async_copy(source, target, in_sem.at[i])
        for i, (source, target) in enumerate((
            (rows_hbm, rows_ref),
            (cols_hbm, cols_ref),
            (count_hbm, count_ref),
            (x_hbm, pieces[0]),
            (w_hbm, w_ref),
        ))
    ]
    for fetch in fetches:
        fetch.start()

    def load(turn):
        j = flip(blk, back(turn, n_blk), n_blk)
        return pltpu.make_async_copy(vals_hbm.at[j], vals[turn], vals_sem.at[turn])

    load(0).start()

    peers = len(direct) + 1 + jnp.where(place > 0, 1, 0) + jnp.where(place < line - 1, 1, 0)
    pl.semaphore_wait(barrier, peers)

    def half(ref, h):
        return ref.at[:, pl.ds(h * (BS // 2), BS // 2)]

    def pass_on(source, turn, h, to):
        return pltpu.make_async_remote_copy(
            src_ref=half(source, h),
            dst_ref=half(pieces[turn], h),
            send_sem=x_send_sem.at[turn, h],
            recv_sem=x_recv_sem.at[turn, h],
            device_id={"blk": flip(blk, to, n_blk)},
            device_id_type=MESH,
        )

    sends = [
        pass_on(x_hbm, turn, (first + turn + 1) % 2, turn) for first in (0, 1) for turn in direct
    ]
    for send in sends:
        send.start()
    for turn in range(1, n_blk):
        load(turn).start()

    prep[...] = jnp.zeros(prep.shape, jnp.int32)
    for fetch in fetches[:3]:
        fetch.wait()

    def index(turn):
        j = flip(blk, back(turn, n_blk), n_blk)
        prepare(
            rows_ref[pl.ds(j, 1), :], cols_ref[pl.ds(j, 1), :], count_ref[0, j],
            prep.at[turn], turn * slots, n_blk * slots, group * 2 * line, group,
        )

    fills = [
        pltpu.make_async_copy(prep.at[turn], table.at[turn], table_sem.at[turn])
        for turn in range(n_blk)
    ]
    index(0)
    fills[0].start()
    chain[n_blk * slots] = jnp.zeros((BS, width), jnp.float32)

    fills[0].wait()
    for fetch in fetches[3:]:
        fetch.wait()
    batch = max(u for u in range(1, 41) if slots % u == 0)
    lower = place < line // 2

    def early_sum(k):
        total = chain[table[0, 3, k]]
        for turn in range(1, n_blk - 1):
            total = total + chain[table[turn, 3, k]]
        return total

    def last_sum(k):
        return chain[table[n_blk - 1, 3, k]]

    def early(d, carry):
        for g in range(group):
            at = (d, pl.ds(g * BS, BS))
            sib_send[at] = early_sum((2 * d + 1 - core) * group + g)
            own[at] = early_sum((2 * d + core) * group + g)
        return carry

    for turn in range(n_blk):
        if turn == n_blk - 1:
            lax.fori_loop(0, line, early, 0)
        if square and turn == 1:
            for near, h in ((1, 0), (2, 1)):
                pass_on(x_hbm, near, h, near).wait_recv()
                onward = pass_on(pieces[near], 3, h, 3 - near)
                onward.start()
                sends.append(onward)
        load(turn).wait()
        for h in (0, 1) if turn else ():
            if not (square and h == turn - 1):
                pass_on(x_hbm, turn, h, direct[0]).wait_recv()

        if turn:
            fills[turn].wait()

        def some(g, total, j=turn, piece=pieces[turn], blocks=vals[turn]):
            for u in range(batch):
                t = g * batch + u
                product = jnp.dot(
                    blocks[table[j, 0, t]],
                    piece[table[j, 1, t]],
                    preferred_element_type=jnp.float32,
                )
                total = total * table[j, 2, t].astype(jnp.float32) + product
                chain[j * slots + t] = total
            return total

        if turn == 0:
            for later in range(1, n_blk):
                index(later)
        total = jnp.zeros((BS, width), jnp.float32)
        if slots == batch:
            some(0, total)
        else:
            lax.fori_loop(0, slots // batch, some, total)
        if turn == 0:
            for later in range(1, n_blk):
                fills[later].start()

    def sib_copy(d):
        return pltpu.make_async_remote_copy(
            src_ref=sib_send.at[d],
            dst_ref=sib_recv.at[d],
            send_sem=sib_send_sem.at[d],
            recv_sem=sib_recv_sem.at[d],
            device_id=sibling,
            device_id_type=MESH,
        )

    def order(i):
        return jnp.where(lower, line - 1 - i, i)

    def gather(i, carry):
        d = order(i)
        for g in range(group):
            at = (d, pl.ds(g * BS, BS))
            sib_send[at] = sib_send[at] + last_sum((2 * d + 1 - core) * group + g)

        @pl.when(i == 0)
        def _():
            sib_copy(d).start()

        for g in range(group):
            at = (d, pl.ds(g * BS, BS))
            own[at] = own[at] + last_sum((2 * d + core) * group + g)
        return carry

    def cross(i, carry):
        sib_copy(order(i)).start()
        return carry

    lax.fori_loop(0, line, gather, 0)

    def rows_of(g):
        return pl.ds(0, PAD + BS) if g == 0 else pl.ds(PAD + g * BS, BS)

    def up_copy(d, g):
        return pltpu.make_async_remote_copy(
            src_ref=box_send.at[d, rows_of(g)],
            dst_ref=up_recv.at[d, rows_of(g)],
            send_sem=box_send_sem.at[d, g],
            recv_sem=up_sem.at[d, g],
            device_id=above,
            device_id_type=MESH,
        )

    def down_copy(d, g):
        return pltpu.make_async_remote_copy(
            src_ref=box_send.at[d, rows_of(g)],
            dst_ref=down_recv.at[d, rows_of(g)],
            send_sem=box_send_sem.at[d, g],
            recv_sem=down_sem.at[d, g],
            device_id=below,
            device_id_type=MESH,
        )

    def hop(d, copy, box, first):
        sib_copy(d).wait_recv()
        both = own[d] + sib_recv[d]
        own[d] = both
        top = jnp.max(jnp.abs(both), axis=0, keepdims=True)
        if not first:
            copy(d, 0).wait_recv()
            scale = scale_of(read_code(box.at[d]))
            top = top + scale
        code = jnp.ceil(jnp.log2(jnp.maximum(top, TINY)) * STEPS)
        inverse = 1.0 / scale_of(code)
        box_send[d, 0:PAD] = (
            jnp.broadcast_to(code, (PAD, width)).astype(jnp.int32).astype(jnp.int16)
        )
        for g in range(group):
            total = own[d, g * BS:(g + 1) * BS]
            if not first:
                if g:
                    copy(d, g).wait_recv()
                total = total + decode(box.at[d], g, scale)
            whole = jnp.round(total * inverse * LEVELS).astype(jnp.int32)
            box_send[d, PAD + g * BS:PAD + (g + 1) * BS] = whole.astype(jnp.int16)
            copy(d, g).start()

    def step(s, carry):
        up_to = line - 1 - s + place
        down_to = s - (line - 1) + place

        @pl.when(jnp.logical_and(place <= s, place == 0))
        def _():
            hop(up_to, up_copy, up_recv, True)

        @pl.when(jnp.logical_and(place <= s, place > 0))
        def _():
            hop(up_to, up_copy, up_recv, False)

        @pl.when(jnp.logical_and(line - 1 - place <= s, place == line - 1))
        def _():
            hop(down_to, down_copy, down_recv, True)

        @pl.when(jnp.logical_and(line - 1 - place <= s, place < line - 1))
        def _():
            hop(down_to, down_copy, down_recv, False)

        return carry

    if line > 1:
        step(0, 0)
    lax.fori_loop(1, line, cross, 0)
    lax.fori_loop(1, line - 1, step, 0)

    sib_copy(place).wait_recv()
    own[place] = own[place] + sib_recv[place]
    w = w_ref[...]
    for g in range(group):
        block = pl.ds(g * BS, BS)

        @pl.when(place > 0)
        def _():
            up_copy(place, g).wait_recv()
            scale = scale_of(read_code(up_recv.at[place]))
            own[place, block] = own[place, block] + decode(up_recv.at[place], g, scale)

        @pl.when(place < line - 1)
        def _():
            down_copy(place, g).wait_recv()
            scale = scale_of(read_code(down_recv.at[place]))
            own[place, block] = own[place, block] + decode(down_recv.at[place], g, scale)

        total = own[place, block]
        high = total.astype(jnp.bfloat16)
        low = (total - high.astype(jnp.float32)).astype(jnp.bfloat16)
        result = jnp.dot(high, w, preferred_element_type=jnp.float32) + jnp.dot(
            low, w, preferred_element_type=jnp.float32
        )
        out_ref[block] = jnp.maximum(result, 0.0).astype(jnp.bfloat16)

    for send in sends:
        send.wait_send()

    def finish(d, carry):
        sib_copy(d).wait_send()

        @pl.when(d > place)
        def _():
            for g in range(group):
                up_copy(d, g).wait_send()

        @pl.when(d < place)
        def _():
            for g in range(group):
                down_copy(d, g).wait_send()

        return carry

    lax.fori_loop(0, line, finish, 0)


def local(node_feats, block_vals, block_rows, block_cols, block_count, weight):
    n_blk = lax.axis_size("blk")
    line = lax.axis_size("rep") // 2
    width = node_feats.shape[1]
    x = node_feats.reshape(-1, BS, width)
    group = x.shape[0]
    vals = block_vals[0, 0]
    rows = block_rows[0, 0]
    cols = block_cols[0, 0]
    count = block_count[0]
    slots = rows.shape[1]
    unit = group * BS
    vmem = pl.BlockSpec(memory_space=pltpu.VMEM)
    far = pl.BlockSpec(memory_space=pltpu.HBM)
    operands = (x, vals, rows, cols, count, weight)
    dma = pltpu.SemaphoreType.DMA
    scratch = [
        pltpu.VMEM(rows.shape, jnp.int32),
        pltpu.VMEM(cols.shape, jnp.int32),
        pltpu.SMEM(count.shape, jnp.int32),
        pltpu.VMEM(weight.shape, jnp.bfloat16),
        pltpu.VMEM((n_blk, 8, 128), jnp.int32),
        pltpu.SMEM((n_blk, 8, 128), jnp.int32),
        pltpu.VMEM((n_blk * slots + 1, BS, width), jnp.float32),
        pltpu.VMEM((line, unit, width), jnp.float32),
        pltpu.VMEM((line, unit, width), jnp.float32),
        pltpu.VMEM((line, unit, width), jnp.float32),
        pltpu.VMEM((line, unit + PAD, width), jnp.int16),
        pltpu.VMEM((line, unit + PAD, width), jnp.int16),
        pltpu.VMEM((line, unit + PAD, width), jnp.int16),
    ]
    semaphores = [
        dma((n_blk,)), dma((n_blk, 2)), dma((n_blk, 2)),
        dma((line,)), dma((line,)),
        dma((line, group)), dma((line, group)), dma((line, group)),
        dma((n_blk,)), dma((5,)),
    ]
    landing = [pltpu.VMEM((group, BS, width), jnp.bfloat16)] * n_blk
    landing += [pltpu.VMEM(vals.shape[1:], jnp.bfloat16)] * n_blk
    used = sum(
        math.prod(ref.shape) * jnp.dtype(ref.dtype).itemsize
        for ref in scratch + landing
    )
    return pl.pallas_call(
        functools.partial(kernel, n_blk, line, group),
        out_shape=jax.ShapeDtypeStruct((unit, weight.shape[1]), jnp.bfloat16),
        in_specs=[far] * 6,
        out_specs=vmem,
        scratch_shapes=scratch + semaphores + landing,
        compiler_params=pltpu.CompilerParams(
            collective_id=0, has_side_effects=True, vmem_limit_bytes=used + 4 * 1024 * 1024
        ),
        cost_estimate=pl.CostEstimate(
            flops=2 * n_blk * slots * BS * BS * width,
            bytes_accessed=2 * n_blk * slots * BS * BS,
            transcendentals=0,
        ),
    )(*(pltpu.with_memory_space_constraint(a, pltpu.HBM) for a in operands))


def solution(mesh):
    return jax.shard_map(
        local,
        mesh=mesh,
        in_specs=(
            P(("blk", "rep"), None),
            P("blk", "rep", None, None, None, None),
            P("blk", "rep", None, None),
            P("blk", "rep", None, None),
            P("blk", "rep", None),
            P(),
        ),
        out_specs=P(("blk", "rep"), None),
        check_vma=False,
    )
```

```python
import functools
import math

import jax
import jax.numpy as jnp
from jax import lax
from jax.experimental import pallas as pl
from jax.experimental.pallas import tpu as pltpu
from jax.sharding import PartitionSpec as P

BS = 128
LEVELS = 32000.0
STEPS = 256.0
TINY = 1e-36
PAD = 16
MESH = pl.DeviceIdType.MESH


def flip(index, mask, size):
    if size & (size - 1):
        return (index + mask) % size
    out = index
    bit = 1
    while bit < size:
        if mask & bit:
            out = out + bit * (1 - 2 * ((index // bit) % 2))
        bit *= 2
    return out


def back(mask, size):
    return (size - mask) % size if size & (size - 1) else mask


def scale_of(code):
    return jnp.exp2(code * (1.0 / STEPS))


def read_code(box):
    return box[pl.ds(0, PAD)].astype(jnp.int32).astype(jnp.float32)[0:1]


def decode(box, g, scale):
    part = box[pl.ds(PAD + g * BS, BS)].astype(jnp.int32).astype(jnp.float32)
    return part * (1.0 / LEVELS) * scale


def prepare(rows, cols, live_count, prep, base, nothing, panel, group):
    slots = rows.shape[1]
    lane = lax.broadcasted_iota(jnp.int32, (slots, slots), 1)
    sub = lax.broadcasted_iota(jnp.int32, (slots, slots), 0)
    place = lax.broadcasted_iota(jnp.int32, (slots, panel), 1)
    col_bits = max(1, (group - 1).bit_length())
    slot_bits = max(1, (slots - 1).bit_length())
    row_bits = col_bits + slot_bits

    live = lane[0:1] < live_count
    key = jnp.where(live, rows, panel)
    col = jnp.where(live, cols, 0)
    word = key * (1 << row_bits) + lane[0:1] * (1 << col_bits) + col
    spread = jnp.broadcast_to(word, (slots, slots))
    word_up = jnp.sum(jnp.where(lane == sub, spread, 0), axis=1, keepdims=True)
    rank = jnp.sum(jnp.where(word < word_up, 1, 0), axis=1, keepdims=True)
    key_up = word_up >> row_bits
    before = jnp.max(jnp.where(rank == lane - 1, key_up, -1), axis=0, keepdims=True)
    ordered = jnp.sum(jnp.where(rank == lane, word_up, 0), axis=0, keepdims=True)
    prep[0:1, 0:slots] = (ordered >> col_bits) & ((1 << slot_bits) - 1)
    prep[1:2, 0:slots] = ordered & ((1 << col_bits) - 1)
    prep[2:3, 0:slots] = jnp.where(before == (ordered >> row_bits), 1, 0)
    upto = jnp.sum(jnp.where(key_up <= place, 1, 0), axis=0, keepdims=True)
    found = jnp.max(jnp.where(key_up == place, 1, 0), axis=0, keepdims=True)
    prep[3:4, 0:panel] = jnp.where(found > 0, upto + (base - 1), nothing)


def kernel(
    n_blk, line, group,
    x_hbm, vals_hbm, rows_hbm, cols_hbm, count_hbm, w_hbm, out_ref,
    rows_ref, cols_ref, count_ref, w_ref, prep, table, chain, own, sib_send, sib_recv, box_send, up_recv, down_recv,
    vals_sem, x_send_sem, x_recv_sem, sib_send_sem, sib_recv_sem,
    box_send_sem, up_sem, down_sem, table_sem, in_sem, *pieces_and_vals,
):
    pieces = pieces_and_vals[:n_blk]
    vals = pieces_and_vals[n_blk:]
    slots = vals_hbm.shape[1]
    width = x_hbm.shape[2]
    blk = lax.axis_index("blk")
    rep = lax.axis_index("rep")
    place = rep // 2
    core = rep % 2
    sibling = {"rep": place * 2 + 1 - core}
    above = {"rep": rep + 2}
    below = {"rep": rep - 2}

    square = n_blk == 4
    direct = (1, 2) if square else tuple(range(1, n_blk))

    barrier = pltpu.get_barrier_semaphore()
    for turn in direct:
        pl.semaphore_signal(
            barrier, inc=1, device_id={"blk": flip(blk, turn, n_blk)}, device_id_type=MESH
        )
    pl.semaphore_signal(barrier, inc=1, device_id=sibling, device_id_type=MESH)

    @pl.when(place < line - 1)
    def _():
        pl.semaphore_signal(barrier, inc=1, device_id=above, device_id_type=MESH)

    @pl.when(place > 0)
    def _():
        pl.semaphore_signal(barrier, inc=1, device_id=below, device_id_type=MESH)

    fetches = [
        pltpu.make_async_copy(source, target, in_sem.at[i])
        for i, (source, target) in enumerate((
            (rows_hbm, rows_ref),
            (cols_hbm, cols_ref),
            (count_hbm, count_ref),
            (x_hbm, pieces[0]),
            (w_hbm, w_ref),
        ))
    ]
    for fetch in fetches:
        fetch.start()

    def load(turn):
        j = flip(blk, back(turn, n_blk), n_blk)
        return pltpu.make_async_copy(vals_hbm.at[j], vals[turn], vals_sem.at[turn])

    load(0).start()

    peers = len(direct) + 1 + jnp.where(place > 0, 1, 0) + jnp.where(place < line - 1, 1, 0)
    pl.semaphore_wait(barrier, peers)

    def half(ref, h):
        return ref.at[:, pl.ds(h * (BS // 2), BS // 2)]

    def pass_on(source, turn, h, to):
        return pltpu.make_async_remote_copy(
            src_ref=half(source, h),
            dst_ref=half(pieces[turn], h),
            send_sem=x_send_sem.at[turn, h],
            recv_sem=x_recv_sem.at[turn, h],
            device_id={"blk": flip(blk, to, n_blk)},
            device_id_type=MESH,
        )

    sends = [
        pass_on(x_hbm, turn, (first + turn + 1) % 2, turn) for first in (0, 1) for turn in direct
    ]
    for send in sends:
        send.start()
    for turn in range(1, n_blk):
        load(turn).start()

    prep[...] = jnp.zeros(prep.shape, jnp.int32)
    for fetch in fetches[:3]:
        fetch.wait()

    def index(turn):
        j = flip(blk, back(turn, n_blk), n_blk)
        prepare(
            rows_ref[pl.ds(j, 1), :], cols_ref[pl.ds(j, 1), :], count_ref[0, j],
            prep.at[turn], turn * slots, n_blk * slots, group * 2 * line, group,
        )

    fills = [
        pltpu.make_async_copy(prep.at[turn], table.at[turn], table_sem.at[turn])
        for turn in range(n_blk)
    ]
    index(0)
    fills[0].start()
    chain[n_blk * slots] = jnp.zeros((BS, width), jnp.float32)

    fills[0].wait()
    for fetch in fetches[3:]:
        fetch.wait()
    batch = max(u for u in range(2, 41, 2) if slots % u == 0)
    lower = place < line // 2

    def early_sum(k):
        total = chain[table[0, 3, k]]
        for turn in range(1, n_blk - 1):
            total = total + chain[table[turn, 3, k]]
        return total

    def last_sum(k):
        return chain[table[n_blk - 1, 3, k]]

    def early(d, carry):
        for g in range(group):
            at = (d, pl.ds(g * BS, BS))
            sib_send[at] = early_sum((2 * d + 1 - core) * group + g)
            own[at] = early_sum((2 * d + core) * group + g)
        return carry

    for turn in range(n_blk):
        if turn == n_blk - 1:
            lax.fori_loop(0, line, early, 0)
        if square and turn == 1:
            for near, h in ((1, 0), (2, 1)):
                pass_on(x_hbm, near, h, near).wait_recv()
                onward = pass_on(pieces[near], 3, h, 3 - near)
                onward.start()
                sends.append(onward)
        load(turn).wait()
        for h in (0, 1) if turn else ():
            if not (square and h == turn - 1):
                pass_on(x_hbm, turn, h, direct[0]).wait_recv()

        if turn:
            fills[turn].wait()

        def some(g, total, j=turn, piece=pieces[turn], blocks=vals[turn]):
            for u in range(0, batch, 2):
                t = g * batch + u
                left = [blocks[table[j, 0, t + v]] for v in (0, 1)]
                right = [piece[table[j, 1, t + v]] for v in (0, 1)]
                none = jnp.zeros_like(right[0])
                both = jnp.dot(
                    jnp.concatenate(left, axis=1),
                    jnp.concatenate(
                        [
                            jnp.concatenate([right[0], none], axis=1),
                            jnp.concatenate([none, right[1]], axis=1),
                        ],
                        axis=0,
                    ),
                    preferred_element_type=jnp.float32,
                )
                for v in (0, 1):
                    product = both[:, v * width:(v + 1) * width]
                    total = total * table[j, 2, t + v].astype(jnp.float32) + product
                    chain[j * slots + t + v] = total
            return total

        if turn == 0:
            for later in range(1, n_blk):
                index(later)
        total = jnp.zeros((BS, width), jnp.float32)
        if slots == batch:
            some(0, total)
        else:
            lax.fori_loop(0, slots // batch, some, total)
        if turn == 0:
            for later in range(1, n_blk):
                fills[later].start()

    def sib_copy(d):
        return pltpu.make_async_remote_copy(
            src_ref=sib_send.at[d],
            dst_ref=sib_recv.at[d],
            send_sem=sib_send_sem.at[d],
            recv_sem=sib_recv_sem.at[d],
            device_id=sibling,
            device_id_type=MESH,
        )

    def gather(i, carry):
        d = jnp.where(lower, line - 1 - i, i)
        for g in range(group):
            at = (d, pl.ds(g * BS, BS))
            sib_send[at] = sib_send[at] + last_sum((2 * d + 1 - core) * group + g)
        sib_copy(d).start()
        for g in range(group):
            at = (d, pl.ds(g * BS, BS))
            own[at] = own[at] + last_sum((2 * d + core) * group + g)
        return carry

    lax.fori_loop(0, line, gather, 0)

    def rows_of(g):
        return pl.ds(0, PAD + BS) if g == 0 else pl.ds(PAD + g * BS, BS)

    def up_copy(d, g):
        return pltpu.make_async_remote_copy(
            src_ref=box_send.at[d, rows_of(g)],
            dst_ref=up_recv.at[d, rows_of(g)],
            send_sem=box_send_sem.at[d, g],
            recv_sem=up_sem.at[d, g],
            device_id=above,
            device_id_type=MESH,
        )

    def down_copy(d, g):
        return pltpu.make_async_remote_copy(
            src_ref=box_send.at[d, rows_of(g)],
            dst_ref=down_recv.at[d, rows_of(g)],
            send_sem=box_send_sem.at[d, g],
            recv_sem=down_sem.at[d, g],
            device_id=below,
            device_id_type=MESH,
        )

    def hop(d, copy, box, first):
        sib_copy(d).wait_recv()
        both = own[d] + sib_recv[d]
        own[d] = both
        top = jnp.max(jnp.abs(both), axis=0, keepdims=True)
        if not first:
            copy(d, 0).wait_recv()
            scale = scale_of(read_code(box.at[d]))
            top = top + scale
        code = jnp.ceil(jnp.log2(jnp.maximum(top, TINY)) * STEPS)
        inverse = 1.0 / scale_of(code)
        box_send[d, 0:PAD] = (
            jnp.broadcast_to(code, (PAD, width)).astype(jnp.int32).astype(jnp.int16)
        )
        for g in range(group):
            total = own[d, g * BS:(g + 1) * BS]
            if not first:
                if g:
                    copy(d, g).wait_recv()
                total = total + decode(box.at[d], g, scale)
            whole = jnp.round(total * inverse * LEVELS).astype(jnp.int32)
            box_send[d, PAD + g * BS:PAD + (g + 1) * BS] = whole.astype(jnp.int16)
            copy(d, g).start()

    def step(s, carry):
        up_to = line - 1 - s + place
        down_to = s - (line - 1) + place

        @pl.when(jnp.logical_and(place <= s, place == 0))
        def _():
            hop(up_to, up_copy, up_recv, True)

        @pl.when(jnp.logical_and(place <= s, place > 0))
        def _():
            hop(up_to, up_copy, up_recv, False)

        @pl.when(jnp.logical_and(line - 1 - place <= s, place == line - 1))
        def _():
            hop(down_to, down_copy, down_recv, True)

        @pl.when(jnp.logical_and(line - 1 - place <= s, place < line - 1))
        def _():
            hop(down_to, down_copy, down_recv, False)

        return carry

    lax.fori_loop(0, line - 1, step, 0)

    sib_copy(place).wait_recv()
    own[place] = own[place] + sib_recv[place]
    w = w_ref[...]
    for g in range(group):
        block = pl.ds(g * BS, BS)

        @pl.when(place > 0)
        def _():
            up_copy(place, g).wait_recv()
            scale = scale_of(read_code(up_recv.at[place]))
            own[place, block] = own[place, block] + decode(up_recv.at[place], g, scale)

        @pl.when(place < line - 1)
        def _():
            down_copy(place, g).wait_recv()
            scale = scale_of(read_code(down_recv.at[place]))
            own[place, block] = own[place, block] + decode(down_recv.at[place], g, scale)

        total = own[place, block]
        high = total.astype(jnp.bfloat16)
        low = (total - high.astype(jnp.float32)).astype(jnp.bfloat16)
        result = jnp.dot(high, w, preferred_element_type=jnp.float32) + jnp.dot(
            low, w, preferred_element_type=jnp.float32
        )
        out_ref[block] = jnp.maximum(result, 0.0).astype(jnp.bfloat16)

    for send in sends:
        send.wait_send()

    def finish(d, carry):
        sib_copy(d).wait_send()

        @pl.when(d > place)
        def _():
            for g in range(group):
                up_copy(d, g).wait_send()

        @pl.when(d < place)
        def _():
            for g in range(group):
                down_copy(d, g).wait_send()

        return carry

    lax.fori_loop(0, line, finish, 0)


def local(node_feats, block_vals, block_rows, block_cols, block_count, weight):
    n_blk = lax.axis_size("blk")
    line = lax.axis_size("rep") // 2
    width = node_feats.shape[1]
    x = node_feats.reshape(-1, BS, width)
    group = x.shape[0]
    vals = block_vals[0, 0]
    rows = block_rows[0, 0]
    cols = block_cols[0, 0]
    count = block_count[0]
    slots = rows.shape[1]
    unit = group * BS
    vmem = pl.BlockSpec(memory_space=pltpu.VMEM)
    far = pl.BlockSpec(memory_space=pltpu.HBM)
    operands = (x, vals, rows, cols, count, weight)
    dma = pltpu.SemaphoreType.DMA
    scratch = [
        pltpu.VMEM(rows.shape, jnp.int32),
        pltpu.VMEM(cols.shape, jnp.int32),
        pltpu.SMEM(count.shape, jnp.int32),
        pltpu.VMEM(weight.shape, jnp.bfloat16),
        pltpu.VMEM((n_blk, 8, 128), jnp.int32),
        pltpu.SMEM((n_blk, 8, 128), jnp.int32),
        pltpu.VMEM((n_blk * slots + 1, BS, width), jnp.float32),
        pltpu.VMEM((line, unit, width), jnp.float32),
        pltpu.VMEM((line, unit, width), jnp.float32),
        pltpu.VMEM((line, unit, width), jnp.float32),
        pltpu.VMEM((line, unit + PAD, width), jnp.int16),
        pltpu.VMEM((line, unit + PAD, width), jnp.int16),
        pltpu.VMEM((line, unit + PAD, width), jnp.int16),
    ]
    semaphores = [
        dma((n_blk,)), dma((n_blk, 2)), dma((n_blk, 2)),
        dma((line,)), dma((line,)),
        dma((line, group)), dma((line, group)), dma((line, group)),
        dma((n_blk,)), dma((5,)),
    ]
    landing = [pltpu.VMEM((group, BS, width), jnp.bfloat16)] * n_blk
    landing += [pltpu.VMEM(vals.shape[1:], jnp.bfloat16)] * n_blk
    used = sum(
        math.prod(ref.shape) * jnp.dtype(ref.dtype).itemsize
        for ref in scratch + landing
    )
    return pl.pallas_call(
        functools.partial(kernel, n_blk, line, group),
        out_shape=jax.ShapeDtypeStruct((unit, weight.shape[1]), jnp.bfloat16),
        in_specs=[far] * 6,
        out_specs=vmem,
        scratch_shapes=scratch + semaphores + landing,
        compiler_params=pltpu.CompilerParams(
            collective_id=0, has_side_effects=True, vmem_limit_bytes=used + 4 * 1024 * 1024
        ),
        cost_estimate=pl.CostEstimate(
            flops=2 * n_blk * slots * BS * BS * width,
            bytes_accessed=2 * n_blk * slots * BS * BS,
            transcendentals=0,
        ),
    )(*(pltpu.with_memory_space_constraint(a, pltpu.HBM) for a in operands))


def solution(mesh):
    return jax.shard_map(
        local,
        mesh=mesh,
        in_specs=(
            P(("blk", "rep"), None),
            P("blk", "rep", None, None, None, None),
            P("blk", "rep", None, None),
            P("blk", "rep", None, None),
            P("blk", "rep", None),
            P(),
        ),
        out_specs=P(("blk", "rep"), None),
        check_vma=False,
    )
```
